128 devices in a mesh: dp: 8 (over z, core), mp: 16 (over x, y).
Axes of the slice: x: 4, y: 4, z: 4, core: 2. Of those that a mesh axis runs over, the one named last changes fastest.
Arguments:
- rhs: float32 [4096, 128], P(('dp', 'mp')), may hold values from -24 to 24
- blocks: bfloat16 [8, 16, 384, 128, 128], P('dp', 'mp'), may hold values from -0.5 to 0.5
- block_rows: int32 [8, 16, 384], P('dp', 'mp'), may hold values from 0 to 511
- block_cols: int32 [8, 16, 384], P('dp', 'mp'), may hold values from 0 to 767
- counts: int32 [8, 16], P('dp', 'mp'), may hold values from 128 to 384, as said below
Outputs:
- solution: float32 [12288, 128], P(('mp', 'dp'))
The draws below stay inside these ranges and needn't reach their ends.
Inputs may be any that keep to these rules, and one draw needn't show every extreme that they name: `counts`: one tile holds exactly 384 live slots and one exactly 128; slots at or beyond a tile's count hold entries that are not used.
All inputs are finite; a program needn't handle non-finite values.
Results may differ from the reference program's by a relative error of at most 0.009.
Values may be sent and summed in bfloat16 or wider, within the bound.
No kernel may reach another device: no remote copies, remote signals or barrier semaphores. Data moves between devices by JAX's collectives and lax.ppermute only.
A program may use at most 64 MiB of HBM per device.

```python
import jax
import jax.numpy as jnp
from jax import lax

BS = 128
KT = 384
RB = 512
CB = 768
ITERS = 2
MROWS = 4096
N_DP = 8
N_MP = 16


def draw_counts(key, part):
    key = jax.random.fold_in(key, 7)
    first_key, second_key = jax.random.split(key)
    values = jax.random.randint(first_key, (N_DP * N_MP,), KT // 3, KT + 1)
    chosen = jax.random.permutation(second_key, N_DP * N_MP)
    values = values.at[chosen[0]].set(KT).at[chosen[1]].set(KT // 3)
    return values.reshape(N_DP, N_MP).astype(jnp.int32)


def touch_ends(values, key, smallest, largest):
    longest = values.shape.index(max(values.shape))
    spots = []
    for shift in (0, 1):
        where = [jax.random.randint(jax.random.fold_in(key, axis), (), 0, length) for axis, length in enumerate(values.shape)]
        where[longest] = (where[longest] + shift) % values.shape[longest]
        spots.append(tuple(where))
    return values.at[spots[0]].set(smallest).at[spots[1]].set(largest)


def levels(rng, extent, pieces, smallest, high):
    gain = 1.0
    for dim, blocks in pieces:
        heights = jax.random.uniform(jax.random.fold_in(jax.random.fold_in(rng, 6), dim), (blocks,), jnp.float32, smallest / len(pieces), high / len(pieces))
        gain = gain * jnp.repeat(jnp.exp(heights), extent[dim] // blocks).reshape((-1,) + (1,) * (len(extent) - 1 - dim))
    return gain


def normal_values(key, extent, deviation, reach, pieces=(), held_as=jnp.bfloat16):
    entries = jax.random.normal(key, extent, jnp.float32) * deviation
    if len(pieces) > 0:
        entries = levels(key, extent, pieces, -0.22, 0.18) * entries
    return jnp.clip(entries, min=-reach, max=reach).astype(held_as)


def setup_inputs(seed: int = 0) -> dict:
    splits = jax.random.split(jax.random.key(seed), 6)
    return {
        "rhs": normal_values(splits[0], (MROWS, BS), 4.0, 24.0, ((0, 128),), jnp.float32),
        "blocks": normal_values(splits[1], (N_DP, N_MP, KT, BS, BS), BS ** -0.5, 0.5, ((0, 8), (1, 16))),
        "block_rows": touch_ends(jax.random.randint(splits[2], (N_DP, N_MP, KT), 0, RB), jax.random.fold_in(splits[2], 1), 0, RB - 1).astype(jnp.int32),
        "block_cols": touch_ends(jax.random.randint(splits[3], (N_DP, N_MP, KT), 0, CB), jax.random.fold_in(splits[3], 1), 0, CB - 1).astype(jnp.int32),
        "counts": draw_counts(jax.random.fold_in(splits[5], 71), 0),
    }


def reference(rhs, blocks, block_rows, block_cols, counts):
    flat_blocks = blocks.reshape(N_DP * N_MP, KT, BS, BS)
    flat_rows = block_rows.reshape(N_DP * N_MP, KT).astype(jnp.int32)
    flat_cols = block_cols.reshape(N_DP * N_MP, KT).astype(jnp.int32)
    flat_counts = counts.reshape(N_DP * N_MP).astype(jnp.int32)
    tile_ids = jnp.arange(N_DP * N_MP, dtype=jnp.int32)
    slot_index = jnp.arange(KT, dtype=jnp.int32)
    row_index = jnp.arange(RB, dtype=jnp.int32)
    col_index = jnp.arange(CB, dtype=jnp.int32)

    def forward(model_vec):
        groups = model_vec.astype(jnp.bfloat16).reshape(N_MP, CB, BS)

        def per_tile(items):
            tile_blocks, slot_rows, slot_cols, live_count, tile_id = items
            picked = groups[tile_id % N_MP][slot_cols].astype(jnp.float32)
            products = jnp.einsum('kab,kb->ka', tile_blocks.astype(jnp.float32), picked, precision=lax.Precision.HIGHEST)
            products = jnp.where((slot_index < live_count)[:, None], products, jnp.zeros_like(products))
            onehot_rows = (slot_rows[None, :] == row_index[:, None]).astype(jnp.float32)
            return jnp.dot(onehot_rows, products, precision=lax.Precision.HIGHEST)
        parts = lax.map(per_tile, (flat_blocks, flat_rows, flat_cols, flat_counts, tile_ids))
        return lax.optimization_barrier(jnp.sum(parts.reshape(N_DP, N_MP, RB, BS), axis=1)).reshape(N_DP * RB, BS)

    def adjoint(data_vec):
        groups = data_vec.astype(jnp.bfloat16).reshape(N_DP, RB, BS)

        def per_tile(items):
            tile_blocks, slot_rows, slot_cols, live_count, tile_id = items
            picked = groups[tile_id // N_MP][slot_rows].astype(jnp.float32)
            products = jnp.einsum('kab,ka->kb', tile_blocks.astype(jnp.float32), picked, precision=lax.Precision.HIGHEST)
            products = jnp.where((slot_index < live_count)[:, None], products, jnp.zeros_like(products))
            onehot_cols = (slot_cols[None, :] == col_index[:, None]).astype(jnp.float32)
            return jnp.dot(onehot_cols, products, precision=lax.Precision.HIGHEST)
        parts = lax.map(per_tile, (flat_blocks, flat_rows, flat_cols, flat_counts, tile_ids))
        return lax.optimization_barrier(jnp.sum(parts.reshape(N_DP, N_MP, CB, BS), axis=0)).reshape(N_MP * CB, BS)

    def length(vector):
        return jnp.sqrt(jnp.sum(vector * vector))
    beta_now = length(rhs)
    data_vec = rhs / beta_now
    model_vec = adjoint(data_vec)
    alpha_now = length(model_vec)
    model_vec = model_vec / alpha_now
    search_dir = model_vec
    solution = jnp.zeros_like(model_vec)
    phi_bar = beta_now
    rho_bar = alpha_now
    for iteration in range(ITERS):
        data_vec = forward(model_vec) - alpha_now * data_vec
        beta_now = length(data_vec)
        data_vec = data_vec / beta_now
        model_vec = adjoint(data_vec) - beta_now * model_vec
        alpha_now = length(model_vec)
        model_vec = model_vec / alpha_now
        rho_now = jnp.sqrt(rho_bar * rho_bar + beta_now * beta_now)
        cosine = rho_bar / rho_now
        sine = beta_now / rho_now
        theta_now = sine * alpha_now
        rho_bar = -cosine * alpha_now
        phi_now = cosine * phi_bar
        phi_bar = sine * phi_bar
        solution = solution + phi_now / rho_now * search_dir
        search_dir = model_vec - theta_now / rho_now * search_dir
    return solution
```

```python
import functools

import jax
import jax.numpy as jnp
from jax import lax
from jax.experimental import pallas as pl
from jax.experimental.pallas import tpu as pltpu
from jax.sharding import PartitionSpec as P

BS = 128
RB = 512
CB = 768
HALF = CB // 2
CHUNK = 96
GROUP = 16
EXTRA = 16
F32 = jnp.float32
BF16 = jnp.bfloat16


def split_rows(value):
    row = lax.broadcasted_iota(jnp.int32, (EXTRA, BS), 0)
    value = jnp.broadcast_to(value, (EXTRA, BS))
    high = value.astype(BF16).astype(F32)
    rest = value - high
    middle = rest.astype(BF16).astype(F32)
    low = rest - middle
    zero = jnp.zeros_like(value)
    return jnp.where(row == 0, high, jnp.where(row == 1, middle, jnp.where(row == 2, low, zero))).astype(BF16)


def joined_rows(rows):
    return jnp.sum(rows.astype(F32), axis=0, keepdims=True)


def square_sum(x):
    return jnp.sum(jnp.sum(x * x, axis=0, keepdims=True), axis=1, keepdims=True)


def column(index):
    pieces = []
    for start in range(0, index.shape[1], BS):
        row = jnp.broadcast_to(index[:, start : start + BS].astype(F32), (BS, BS))
        pieces.append(jnp.transpose(row))
    return jnp.concatenate(pieces, 0)


def gather(source, index):
    at = column(index)
    lane = lax.broadcasted_iota(jnp.int32, at.shape, 1)
    hot = jnp.concatenate(
        [
            jnp.where(at == (lane + start).astype(F32), 1.0, 0.0).astype(BF16)
            for start in range(0, source.shape[0], BS)
        ],
        1,
    )
    return jnp.dot(hot, source, preferred_element_type=F32).astype(BF16)


def scatter(products, index, size, live):
    slots = products.shape[0]
    slot = lax.broadcasted_iota(jnp.int32, (slots, BS), 0)
    products = jnp.where(slot < live, products, 0.0)
    lane = lax.broadcasted_iota(jnp.int32, (size, slots), 1)
    row = lax.broadcasted_iota(jnp.int32, (size, slots), 0)
    hot = jnp.where((jnp.broadcast_to(index, (size, slots)) == row) & (lane < live), 1.0, 0.0).astype(BF16)
    high = products.astype(BF16)
    low = (products - high.astype(F32)).astype(BF16)
    both = jnp.dot(hot, jnp.concatenate([high, low], 1), preferred_element_type=F32)
    return both[:, :BS] + both[:, BS:]


def spread(picked):
    row = lax.broadcasted_iota(jnp.int32, (GROUP, BS), 0)
    wide = picked.astype(F32)
    return jnp.concatenate([jnp.where(row == slot, wide, 0.0).astype(BF16) for slot in range(GROUP)], 1)


def multiply(transposed, blocks_ref, picked_ref, products_ref):
    for start in range(0, picked_ref.shape[0], GROUP):
        picked = spread(picked_ref[start : start + GROUP, :])
        if transposed:
            tile = blocks_ref[start : start + GROUP].reshape(GROUP * BS, BS)
            product = jnp.dot(picked, tile, preferred_element_type=F32)
        else:
            tile = jnp.concatenate([blocks_ref[start + slot] for slot in range(GROUP)], 1)
            product = lax.dot_general(picked, tile, (((1,), (1,)), ((), ())), preferred_element_type=F32)
        products_ref[start : start + GROUP, :] = product


def adjoint_tail(live_ref, data, rows_ref, cols_ref, blocks_ref, keep_ref, send_ref, picked_ref, products_ref):
    picked_ref[...] = gather(data.astype(BF16), rows_ref[...])
    multiply(True, blocks_ref, picked_ref, products_ref)
    partial = scatter(products_ref[...], cols_ref[...], CB, live_ref[0])
    keep_ref[...] = partial[:HALF]
    send_ref[:HALF, :] = partial[HALF:].astype(BF16)
    send_ref[HALF:, :] = split_rows(square_sum(data))


def first_adjoint(
    live_ref, data_ref, rows_ref, cols_ref, blocks_ref, keep_ref, send_ref, picked_ref, products_ref
):
    adjoint_tail(
        live_ref, data_ref[...], rows_ref, cols_ref, blocks_ref, keep_ref, send_ref, picked_ref, products_ref
    )


def forward_sum(own_ref, one_ref, two_ref, three_ref):
    parts = [ref[...].astype(F32) for ref in (own_ref, one_ref, two_ref, three_ref)]
    return (parts[0] + parts[1]) + (parts[2] + parts[3])


def next_data(own_ref, one_ref, two_ref, three_ref, data_ref, beta2_ref):
    whole = forward_sum(own_ref, one_ref, two_ref, three_ref)
    alpha2 = joined_rows(whole[RB:])
    alpha = jnp.sqrt(alpha2)
    beta = jnp.sqrt(beta2_ref[0:1, :])
    return whole[:RB] / alpha - alpha * (data_ref[...] / beta), alpha2


def second_adjoint(
    live_ref,
    own_ref,
    one_ref,
    two_ref,
    three_ref,
    data_ref,
    beta2_ref,
    rows_ref,
    cols_ref,
    blocks_ref,
    next_ref,
    alpha2_ref,
    keep_ref,
    send_ref,
    picked_ref,
    products_ref,
):
    data, alpha2 = next_data(own_ref, one_ref, two_ref, three_ref, data_ref, beta2_ref)
    next_ref[...] = data
    alpha2_ref[...] = jnp.broadcast_to(alpha2, alpha2_ref.shape)
    adjoint_tail(live_ref, data, rows_ref, cols_ref, blocks_ref, keep_ref, send_ref, picked_ref, products_ref)


def chip_sum(keep_ref, send_ref, got_ref, out_ref):
    out_ref[:HALF, :] = (keep_ref[...] + got_ref[:HALF, :].astype(F32)).astype(BF16)
    out_ref[HALF:, :] = split_rows(joined_rows(send_ref[HALF:, :]) + joined_rows(got_ref[HALF:, :]))


def model_sum(own_ref, one_ref, two_ref, three_ref):
    whole = forward_sum(own_ref, one_ref, two_ref, three_ref)
    return whole[:HALF], joined_rows(whole[HALF:])


def model_out(model, beta2, model_ref, send_ref, beta2_ref):
    model_ref[...] = model
    send_ref[:HALF, :] = model.astype(BF16)
    send_ref[HALF:, :] = split_rows(square_sum(model))
    beta2_ref[...] = jnp.broadcast_to(beta2, beta2_ref.shape)


def first_model(own_ref, one_ref, two_ref, three_ref, model_ref, send_ref, beta2_ref):
    total, beta2 = model_sum(own_ref, one_ref, two_ref, three_ref)
    model_out(total / jnp.sqrt(beta2), beta2, model_ref, send_ref, beta2_ref)


def second_model(
    own_ref, one_ref, two_ref, three_ref, last_ref, alpha2_ref, model_ref, send_ref, beta2_ref
):
    total, beta2 = model_sum(own_ref, one_ref, two_ref, three_ref)
    beta = jnp.sqrt(beta2)
    last = last_ref[...] / jnp.sqrt(alpha2_ref[0:1, :])
    model_out(total / beta - beta * last, beta2, model_ref, send_ref, beta2_ref)


def forward(live_ref, own_ref, got_ref, rows_ref, cols_ref, blocks_ref, out_ref, picked_ref, products_ref):
    model = jnp.concatenate([own_ref[:HALF, :], got_ref[:HALF, :]], 0)
    picked_ref[...] = gather(model, cols_ref[...])
    multiply(False, blocks_ref, picked_ref, products_ref)
    out_ref[:RB, :] = scatter(products_ref[...], rows_ref[...], RB, live_ref[0]).astype(BF16)
    out_ref[RB:, :] = split_rows(joined_rows(own_ref[HALF:, :]) + joined_rows(got_ref[HALF:, :]))


def row_sum(own_ref, one_ref, two_ref, three_ref, out_ref):
    whole = forward_sum(own_ref, one_ref, two_ref, three_ref)
    out_ref[:RB, :] = whole[:RB].astype(BF16)
    out_ref[RB:, :] = split_rows(joined_rows(whole[RB:]))


def last_data(own_ref, one_ref, two_ref, three_ref, data_ref, beta2_ref, alpha2_ref, square_ref):
    data, alpha2 = next_data(own_ref, one_ref, two_ref, three_ref, data_ref, beta2_ref)
    alpha2_ref[...] = jnp.broadcast_to(alpha2, alpha2_ref.shape)
    square_ref[...] = jnp.broadcast_to(square_sum(data), square_ref.shape)


def finish(
    place_ref,
    own_ref,
    one_ref,
    two_ref,
    three_ref,
    beta0_ref,
    alpha0_ref,
    beta1_ref,
    alpha1_ref,
    model0_ref,
    model1_ref,
    out_ref,
):
    beta0 = jnp.sqrt(beta0_ref[0:1, :])
    alpha0 = jnp.sqrt(alpha0_ref[0:1, :])
    beta1 = jnp.sqrt(beta1_ref[0:1, :])
    alpha1 = jnp.sqrt(alpha1_ref[0:1, :])
    beta2 = jnp.sqrt(forward_sum(own_ref, one_ref, two_ref, three_ref)[0:1, :])
    chunk = pl.ds(pl.multiple_of(place_ref[0] * CHUNK, CHUNK), CHUNK)
    model0 = model0_ref[chunk, :] / alpha0
    model1 = model1_ref[chunk, :] / alpha1
    rho1 = jnp.sqrt(alpha0 * alpha0 + beta1 * beta1)
    cosine = alpha0 / rho1
    sine = beta1 / rho1
    theta = sine * alpha1
    rho_bar = -cosine * alpha1
    phi1 = cosine * beta0
    phi_bar = sine * beta0
    search = model1 - theta / rho1 * model0
    rho2 = jnp.sqrt(rho_bar * rho_bar + beta2 * beta2)
    phi2 = rho_bar / rho2 * phi_bar
    out_ref[...] = phi1 / rho1 * model0 + phi2 / rho2 * search


SCALAR = pl.BlockSpec(memory_space=pltpu.SMEM)
VECTOR = pl.BlockSpec(memory_space=pltpu.VMEM)


def call(kernel, outs, vectors, scalars=(), slots=0):
    scratch = [pltpu.VMEM((slots, BS), BF16), pltpu.VMEM((slots, BS), F32)] if slots else []
    return pl.pallas_call(
        kernel,
        out_shape=[jax.ShapeDtypeStruct((rows, BS), dtype) for rows, dtype in outs],
        in_specs=[SCALAR] * len(scalars) + [VECTOR] * len(vectors),
        out_specs=[VECTOR] * len(outs),
        scratch_shapes=scratch,
        compiler_params=pltpu.CompilerParams(vmem_limit_bytes=16 * 2**20),
        name=kernel.__name__,
    )(*scalars, *vectors)


def body(rhs, blocks, block_rows, block_cols, counts):
    slots = blocks.shape[2]
    tile = pltpu.with_memory_space_constraint(blocks[0, 0], pltpu.VMEM)
    rows = block_rows[0]
    cols = block_cols[0]
    live = counts[0]
    place = lax.axis_index("dp")
    core = place % 2
    chip = place // 2
    cols = jnp.where((cols // CHUNK) % 2 == core, 0, HALF) + cols // (2 * CHUNK) * CHUNK + cols % CHUNK

    def over_core(x):
        return lax.ppermute(x, "dp", [(i, i ^ 1) for i in range(8)])

    def over_chips(x):
        return [lax.ppermute(x, "dp", [(i, (i + 2 * hop) % 8) for i in range(8)]) for hop in (1, 2, 3)]

    def over_x(x):
        return [lax.ppermute(x, "mp", [(i, (i + 4 * hop) % 16) for i in range(16)]) for hop in (1, 2, 3)]

    def over_y(x):
        return [
            lax.ppermute(x, "mp", [(i, i // 4 * 4 + (i + hop) % 4) for i in range(16)]) for hop in (1, 2, 3)
        ]

    message = (HALF + EXTRA, BF16)
    scalar = (8, F32)
    model_outs = [(HALF, F32), message, scalar]

    def forward_whole(own):
        (part,) = call(forward, [(RB + EXTRA, BF16)], [own, over_core(own), rows, cols, tile], [live], slots)
        (part,) = call(row_sum, [(RB + EXTRA, BF16)], [part, *over_x(part)])
        return [part, *over_y(part)]

    def chips_whole(keep, send):
        (part,) = call(chip_sum, [message], [keep, send, over_core(send)])
        return [part, *over_chips(part)]

    shares = jnp.broadcast_to(rhs[None], (16, *rhs.shape))
    data0 = lax.all_to_all(shares, "mp", 0, 0).reshape(RB, BS)
    keep, send = call(first_adjoint, [(HALF, F32), message], [data0, rows, cols, tile], [live], slots)
    model0, own, beta0 = call(first_model, model_outs, chips_whole(keep, send))
    data1, alpha0, keep, send = call(
        second_adjoint,
        [(RB, F32), scalar, (HALF, F32), message],
        [*forward_whole(own), data0, beta0, rows, cols, tile],
        [live],
        slots,
    )
    model1, own, beta1 = call(second_model, model_outs, [*chips_whole(keep, send), model0, alpha0])
    alpha1, square = call(last_data, [scalar, scalar], [*forward_whole(own), data1, beta1])
    square = square + over_core(square)
    (out,) = call(
        finish,
        [(CHUNK, F32)],
        [square, *over_chips(square), beta0, alpha0, beta1, alpha1, model0, model1],
        [chip[None]],
    )
    return out


def solution(mesh):
    placed = (
        P(("dp", "mp"), None),
        P("dp", "mp", None, None, None),
        P("dp", "mp", None),
        P("dp", "mp", None),
        P("dp", "mp"),
    )
    return jax.shard_map(
        body, mesh=mesh, in_specs=placed, out_specs=P(("mp", "dp"), None), check_vma=False
    )
```

```python
import functools

import jax
import jax.numpy as jnp
from jax import lax
from jax.experimental import pallas as pl
from jax.experimental.pallas import tpu as pltpu
from jax.sharding import PartitionSpec as P

BS = 128
RB = 512
CB = 768
HALF = CB // 2
CHUNK = 96
GROUP = 16
EXTRA = 16
LOADS = 8
SHARE = 32
NEAR = (1, 3)
FAR = (3, 1)
F32 = jnp.float32
BF16 = jnp.bfloat16


def square(other_x, other_y):
    return 4 * other_x, other_y, 4 * other_x + other_y


def split_rows(value):
    row = lax.broadcasted_iota(jnp.int32, (EXTRA, BS), 0)
    value = jnp.broadcast_to(value, (EXTRA, BS))
    high = value.astype(BF16).astype(F32)
    rest = value - high
    middle = rest.astype(BF16).astype(F32)
    low = rest - middle
    zero = jnp.zeros_like(value)
    return jnp.where(row == 0, high, jnp.where(row == 1, middle, jnp.where(row == 2, low, zero))).astype(BF16)


def joined_rows(rows):
    return jnp.sum(rows.astype(F32), axis=0, keepdims=True)


def square_sum(x):
    return jnp.sum(jnp.sum(x * x, axis=0, keepdims=True), axis=1, keepdims=True)


def column(index):
    pieces = []
    for start in range(0, index.shape[1], BS):
        row = jnp.broadcast_to(index[:, start : start + BS].astype(F32), (BS, BS))
        pieces.append(jnp.transpose(row))
    return jnp.concatenate(pieces, 0)


def gather(source, index):
    at = column(index)
    lane = lax.broadcasted_iota(jnp.int32, at.shape, 1)
    hot = jnp.concatenate(
        [
            jnp.where(at == (lane + start).astype(F32), 1.0, 0.0).astype(BF16)
            for start in range(0, source.shape[0], BS)
        ],
        1,
    )
    return jnp.dot(hot, source, preferred_element_type=F32).astype(BF16)


def scatter(products, index, size, live):
    slots = products.shape[0]
    slot = lax.broadcasted_iota(jnp.int32, (slots, BS), 0)
    products = jnp.where(slot < live, products, 0.0)
    lane = lax.broadcasted_iota(jnp.int32, (size, slots), 1)
    row = lax.broadcasted_iota(jnp.int32, (size, slots), 0)
    hot = jnp.where((jnp.broadcast_to(index, (size, slots)) == row) & (lane < live), 1.0, 0.0).astype(BF16)
    high = products.astype(BF16)
    low = (products - high.astype(F32)).astype(BF16)
    both = jnp.dot(hot, jnp.concatenate([high, low], 1), preferred_element_type=F32)
    return both[:, :BS] + both[:, BS:]


def spread(picked):
    row = lax.broadcasted_iota(jnp.int32, (GROUP, BS), 0)
    wide = picked.astype(F32)
    return jnp.concatenate([jnp.where(row == slot, wide, 0.0).astype(BF16) for slot in range(GROUP)], 1)


def multiply(blocks_refs, picked_ref, products_ref):
    base = 0
    for ref in blocks_refs:
        for start in range(0, ref.shape[0], GROUP):
            slots = slice(base + start, base + start + GROUP)
            tile = ref[start : start + GROUP].reshape(GROUP * BS, BS)
            products_ref[slots, :] = jnp.dot(spread(picked_ref[slots, :]), tile, preferred_element_type=F32)
        base += ref.shape[0]


def adjoint_tail(live_ref, data, rows_ref, cols_ref, blocks_refs, keep_ref, send_ref, picked_ref, products_ref):
    picked_ref[...] = gather(data.astype(BF16), rows_ref[...])
    multiply(blocks_refs, picked_ref, products_ref)
    partial = scatter(products_ref[...], cols_ref[...], CB, live_ref[0, 0])
    keep_ref[...] = partial[:HALF]
    send_ref[:HALF, :] = partial[HALF:].astype(BF16)
    send_ref[HALF:, :] = split_rows(square_sum(data))


def first_adjoint(
    live_ref,
    place_ref,
    own_ref,
    one_ref,
    two_ref,
    three_ref,
    rows_ref,
    cols_ref,
    first_ref,
    second_ref,
    data_ref,
    keep_ref,
    send_ref,
    picked_ref,
    products_ref,
):
    near, far = square(*NEAR), square(*FAR)
    for step, ref in zip((0, *far), (own_ref, one_ref, two_ref, three_ref)):
        for piece, hop in enumerate((0, *near)):
            at = pl.multiple_of((place_ref[0] ^ step ^ hop) * SHARE, SHARE)
            data_ref[pl.ds(at, SHARE), :] = ref[piece * SHARE : (piece + 1) * SHARE, :]
    blocks_refs = (first_ref, second_ref)
    adjoint_tail(
        live_ref, data_ref[...], rows_ref, cols_ref, blocks_refs, keep_ref, send_ref, picked_ref, products_ref
    )


def forward_sum(own_ref, one_ref, two_ref, three_ref):
    parts = [ref[...].astype(F32) for ref in (own_ref, one_ref, two_ref, three_ref)]
    return (parts[0] + parts[1]) + (parts[2] + parts[3])


def next_data(own_ref, one_ref, two_ref, three_ref, data_ref, beta2_ref):
    whole = forward_sum(own_ref, one_ref, two_ref, three_ref)
    alpha2 = joined_rows(whole[RB:])
    alpha = jnp.sqrt(alpha2)
    beta = jnp.sqrt(beta2_ref[0:1, :])
    return whole[:RB] / alpha - alpha * (data_ref[...] / beta), alpha2


def second_adjoint(
    live_ref,
    own_ref,
    one_ref,
    two_ref,
    three_ref,
    data_ref,
    beta2_ref,
    rows_ref,
    cols_ref,
    first_ref,
    second_ref,
    next_ref,
    alpha2_ref,
    keep_ref,
    send_ref,
    picked_ref,
    products_ref,
):
    data, alpha2 = next_data(own_ref, one_ref, two_ref, three_ref, data_ref, beta2_ref)
    next_ref[...] = data
    alpha2_ref[...] = jnp.broadcast_to(alpha2, alpha2_ref.shape)
    blocks_refs = (first_ref, second_ref)
    adjoint_tail(live_ref, data, rows_ref, cols_ref, blocks_refs, keep_ref, send_ref, picked_ref, products_ref)


def chip_sum(keep_ref, send_ref, got_ref, out_ref):
    out_ref[:HALF, :] = (keep_ref[...] + got_ref[:HALF, :].astype(F32)).astype(BF16)
    out_ref[HALF:, :] = split_rows(joined_rows(send_ref[HALF:, :]) + joined_rows(got_ref[HALF:, :]))


def model_sum(own_ref, one_ref, two_ref, three_ref):
    whole = forward_sum(own_ref, one_ref, two_ref, three_ref)
    return whole[:HALF], joined_rows(whole[HALF:])


def model_out(model, beta2, model_ref, send_ref, beta2_ref):
    model_ref[...] = model
    send_ref[:HALF, :] = model.astype(BF16)
    send_ref[HALF:, :] = split_rows(square_sum(model))
    beta2_ref[...] = jnp.broadcast_to(beta2, beta2_ref.shape)


def first_model(own_ref, one_ref, two_ref, three_ref, turned_ref, model_ref, send_ref, beta2_ref):
    total, beta2 = model_sum(own_ref, one_ref, two_ref, three_ref)
    model_out(total / jnp.sqrt(beta2), beta2, model_ref, send_ref, beta2_ref)


def second_model(
    own_ref, one_ref, two_ref, three_ref, last_ref, alpha2_ref, model_ref, send_ref, beta2_ref
):
    total, beta2 = model_sum(own_ref, one_ref, two_ref, three_ref)
    beta = jnp.sqrt(beta2)
    last = last_ref[...] / jnp.sqrt(alpha2_ref[0:1, :])
    model_out(total / beta - beta * last, beta2, model_ref, send_ref, beta2_ref)


def forward(live_ref, own_ref, got_ref, rows_ref, cols_ref, blocks_ref, out_ref, picked_ref, products_ref):
    model = jnp.concatenate([own_ref[:HALF, :], got_ref[:HALF, :]], 0)
    picked_ref[...] = gather(model, cols_ref[...])
    multiply((blocks_ref,), picked_ref, products_ref)
    out_ref[:RB, :] = scatter(products_ref[...], rows_ref[...], RB, live_ref[0, 0]).astype(BF16)
    out_ref[RB:, :] = split_rows(joined_rows(own_ref[HALF:, :]) + joined_rows(got_ref[HALF:, :]))


def row_sum(own_ref, one_ref, two_ref, three_ref, out_ref):
    whole = forward_sum(own_ref, one_ref, two_ref, three_ref)
    out_ref[:RB, :] = whole[:RB].astype(BF16)
    out_ref[RB:, :] = split_rows(joined_rows(whole[RB:]))


def last_data(own_ref, one_ref, two_ref, three_ref, data_ref, beta2_ref, alpha2_ref, square_ref):
    data, alpha2 = next_data(own_ref, one_ref, two_ref, three_ref, data_ref, beta2_ref)
    alpha2_ref[...] = jnp.broadcast_to(alpha2, alpha2_ref.shape)
    square_ref[...] = jnp.broadcast_to(square_sum(data), square_ref.shape)


def add(own_ref, got_ref, out_ref):
    out_ref[...] = own_ref[...] + got_ref[...]


def finish(
    chip_ref,
    own_ref,
    one_ref,
    two_ref,
    three_ref,
    beta0_ref,
    alpha0_ref,
    beta1_ref,
    alpha1_ref,
    model0_ref,
    model1_ref,
    out_ref,
):
    beta0 = jnp.sqrt(beta0_ref[0:1, :])
    alpha0 = jnp.sqrt(alpha0_ref[0:1, :])
    beta1 = jnp.sqrt(beta1_ref[0:1, :])
    alpha1 = jnp.sqrt(alpha1_ref[0:1, :])
    beta2 = jnp.sqrt(forward_sum(own_ref, one_ref, two_ref, three_ref)[0:1, :])
    chunk = pl.ds(pl.multiple_of(chip_ref[0] * CHUNK, CHUNK), CHUNK)
    model0 = model0_ref[chunk, :] / alpha0
    model1 = model1_ref[chunk, :] / alpha1
    rho1 = jnp.sqrt(alpha0 * alpha0 + beta1 * beta1)
    cosine = alpha0 / rho1
    sine = beta1 / rho1
    theta = sine * alpha1
    rho_bar = -cosine * alpha1
    phi1 = cosine * beta0
    phi_bar = sine * beta0
    search = model1 - theta / rho1 * model0
    rho2 = jnp.sqrt(rho_bar * rho_bar + beta2 * beta2)
    phi2 = rho_bar / rho2 * phi_bar
    out_ref[...] = phi1 / rho1 * model0 + phi2 / rho2 * search


def read(blocks_ref, tile_ref, sems, first):
    pieces = sems.shape[0]
    size = tile_ref.shape[0] // pieces
    return [
        pltpu.make_async_copy(
            blocks_ref.at[pl.ds(first + piece * size, size)],
            tile_ref.at[pl.ds(piece * size, size)],
            sems.at[piece],
        )
        for piece in range(pieces)
    ]


def load_first(
    core_ref,
    chip_ref,
    place_ref,
    live_ref,
    data_ref,
    rows_ref,
    cols_ref,
    blocks_ref,
    data_out,
    rows_out,
    cols_out,
    tile_ref,
    held_ref,
    small_sems,
    sems,
):
    small = [
        pltpu.make_async_copy(cols_ref, held_ref, small_sems.at[0]),
        pltpu.make_async_copy(rows_ref, rows_out, small_sems.at[1]),
        pltpu.make_async_copy(data_ref, data_out, small_sems.at[2]),
    ]
    large = read(blocks_ref, tile_ref, sems, 0)
    for copy in small + large:
        copy.start()
    small[0].wait()
    cols = held_ref[...]
    chunk = jnp.zeros_like(cols)
    for edge in range(CHUNK, CB, CHUNK):
        chunk += jnp.where(cols >= edge, 1, 0)
    half = jnp.where((chunk & 1) == core_ref[0], 0, HALF)
    cols_out[...] = half + (chunk >> 1) * CHUNK + cols - chunk * CHUNK
    for copy in small[1:] + large:
        copy.wait()


def load_second(after_ref, blocks_ref, tile_ref, sems):
    large = read(blocks_ref, tile_ref, sems, tile_ref.shape[0])
    for copy in large:
        copy.start()
    for copy in large:
        copy.wait()


def transpose(after_ref, first_ref, second_ref, out_ref):
    half = first_ref.shape[0]
    for slot in range(half):
        out_ref[slot] = jnp.transpose(first_ref[slot])
        out_ref[half + slot] = jnp.transpose(second_ref[slot])


def collect(own_ref, one_ref, two_ref, three_ref, after_ref, out_ref):
    size = own_ref.shape[0]
    for piece, ref in enumerate((own_ref, one_ref, two_ref, three_ref)):
        out_ref[piece * size : (piece + 1) * size, :] = ref[...]


SCALAR = pl.BlockSpec(memory_space=pltpu.SMEM)
VECTOR = pl.BlockSpec(memory_space=pltpu.VMEM)


def call(kernel, outs, vectors, scalars=(), slots=0):
    scratch = [pltpu.VMEM((slots, BS), BF16), pltpu.VMEM((slots, BS), F32)] if slots else []
    return pl.pallas_call(
        kernel,
        out_shape=[jax.ShapeDtypeStruct((rows, BS), dtype) for rows, dtype in outs],
        in_specs=[SCALAR] * len(scalars) + [VECTOR] * len(vectors),
        out_specs=[VECTOR] * len(outs),
        scratch_shapes=scratch,
        compiler_params=pltpu.CompilerParams(vmem_limit_bytes=16 * 2**20),
        name=kernel.__name__,
    )(*scalars, *vectors)


def body(rhs, blocks, block_rows, block_cols, counts):
    slots = blocks.shape[2]
    group = lax.axis_index("dp")
    core = (group & 1)[None]
    chip = (group >> 1)[None]
    place = lax.axis_index("mp")[None]

    def over_core(x):
        return lax.ppermute(x, "dp", [(i, i ^ 1) for i in range(8)])

    def over_chips(x):
        return [lax.ppermute(x, "dp", [(i, (i + 2 * hop) % 8) for i in range(8)]) for hop in (1, 2, 3)]

    def over_square(x, others):
        return [lax.ppermute(x, "mp", [(i, i ^ step) for i in range(16)]) for step in square(*others)]

    message = (HALF + EXTRA, BF16)
    scalar = (8, F32)
    model_outs = [(HALF, F32), message, scalar]

    lies = pl.BlockSpec(memory_space=pltpu.HBM)
    inputs = [
        pltpu.with_memory_space_constraint(x, pltpu.HBM) for x in (rhs, block_rows[0], block_cols[0], blocks[0, 0])
    ]
    tile_shape = pltpu.VMEM((slots // 2, BS, BS), BF16)
    params = pltpu.CompilerParams(vmem_limit_bytes=16 * 2**20)
    cost = pl.CostEstimate(flops=0, bytes_accessed=slots * BS * BS * 2, transcendentals=0)
    data, rows, cols, first = pl.pallas_call(
        load_first,
        out_shape=[
            jax.ShapeDtypeStruct(rhs.shape, F32),
            jax.ShapeDtypeStruct((1, slots), jnp.int32),
            jax.ShapeDtypeStruct((1, slots), jnp.int32),
            tile_shape,
        ],
        in_specs=[SCALAR] * 4 + [lies] * 4,
        out_specs=[VECTOR] * 4,
        scratch_shapes=[
            pltpu.VMEM((1, slots), jnp.int32),
            pltpu.SemaphoreType.DMA((3,)),
            pltpu.SemaphoreType.DMA((LOADS,)),
        ],
        compiler_params=params,
        cost_estimate=cost,
        name="load_first",
    )(core, chip, place, counts, *inputs)
    first = pltpu.with_memory_space_constraint(first, pltpu.VMEM)
    (quarter,) = call(collect, [(4 * SHARE, F32)], [data, *over_square(rhs, NEAR), first])
    second = pl.pallas_call(
        load_second,
        out_shape=tile_shape,
        in_specs=[VECTOR, lies],
        out_specs=VECTOR,
        scratch_shapes=[pltpu.SemaphoreType.DMA((LOADS,))],
        compiler_params=params,
        cost_estimate=cost,
        name="load_second",
    )(quarter, inputs[-1])
    second = pltpu.with_memory_space_constraint(second, pltpu.VMEM)

    def forward_whole(own):
        (part,) = call(forward, [(RB + EXTRA, BF16)], [own, over_core(own), rows, cols, turned], [counts], slots)
        (part,) = call(row_sum, [(RB + EXTRA, BF16)], [part, *over_square(part, NEAR)])
        return [part, *over_square(part, FAR)]

    def chips_whole(part):
        return [part, *over_chips(part)]

    data0, keep, send = call(
        first_adjoint,
        [(RB, F32), (HALF, F32), message],
        [quarter, *over_square(quarter, FAR), rows, cols, first, second],
        [counts, place],
        slots,
    )
    (part,) = call(chip_sum, [message], [keep, send, over_core(send)])
    turned = pl.pallas_call(
        transpose,
        out_shape=pltpu.VMEM((slots, BS, BS), BF16),
        in_specs=[VECTOR] * 3,
        out_specs=VECTOR,
        compiler_params=params,
        cost_estimate=cost,
        name="transpose",
    )(part, first, second)
    turned = pltpu.with_memory_space_constraint(turned, pltpu.VMEM)
    model0, own, beta0 = call(first_model, model_outs, [*chips_whole(part), turned])
    data1, alpha0, keep, send = call(
        second_adjoint,
        [(RB, F32), scalar, (HALF, F32), message],
        [*forward_whole(own), data0, beta0, rows, cols, first, second],
        [counts],
        slots,
    )
    (part,) = call(chip_sum, [message], [keep, send, over_core(send)])
    model1, own, beta1 = call(second_model, model_outs, [*chips_whole(part), model0, alpha0])
    alpha1, total = call(last_data, [scalar, scalar], [*forward_whole(own), data1, beta1])
    (total,) = call(add, [scalar], [total, over_core(total)])
    (out,) = call(
        finish,
        [(CHUNK, F32)],
        [total, *over_chips(total), beta0, alpha0, beta1, alpha1, model0, model1],
        [chip],
    )
    return out


def solution(mesh):
    placed = (
        P(("dp", "mp"), None),
        P("dp", "mp", None, None, None),
        P("dp", "mp", None),
        P("dp", "mp", None),
        P("dp", "mp"),
    )
    return jax.shard_map(
        body, mesh=mesh, in_specs=placed, out_specs=P(("mp", "dp"), None), check_vma=False
    )
```

```python
import functools

import jax
import jax.numpy as jnp
from jax import lax
from jax.experimental import pallas as pl
from jax.experimental.pallas import tpu as pltpu
from jax.sharding import PartitionSpec as P

BS = 128
RB = 512
CB = 768
HALF = CB // 2
CHUNK = 96
GROUP = 16
EXTRA = 16
LOADS = 8
SHARE = 32
NEAR = (1, 3)
FAR = (3, 1)
F32 = jnp.float32
BF16 = jnp.bfloat16


def square(other_x, other_y):
    return other_y, 4 * other_x, 4 * other_x + other_y


def split_rows(value):
    row = lax.broadcasted_iota(jnp.int32, (EXTRA, BS), 0)
    value = jnp.broadcast_to(value, (EXTRA, BS))
    high = value.astype(BF16).astype(F32)
    rest = value - high
    middle = rest.astype(BF16).astype(F32)
    low = rest - middle
    zero = jnp.zeros_like(value)
    return jnp.where(row == 0, high, jnp.where(row == 1, middle, jnp.where(row == 2, low, zero))).astype(BF16)


def joined_rows(rows):
    return jnp.sum(rows.astype(F32), axis=0, keepdims=True)


def square_sum(x):
    return jnp.sum(jnp.sum(x * x, axis=0, keepdims=True), axis=1, keepdims=True)


def column(index):
    pieces = []
    for start in range(0, index.shape[1], BS):
        row = jnp.broadcast_to(index[:, start : start + BS].astype(F32), (BS, BS))
        pieces.append(jnp.transpose(row))
    return jnp.concatenate(pieces, 0)


def picker(index, size):
    at = column(index)
    lane = lax.broadcasted_iota(jnp.int32, at.shape, 1)
    return jnp.concatenate(
        [
            jnp.where(at == (lane + start).astype(F32), 1.0, 0.0).astype(BF16)
            for start in range(0, size, BS)
        ],
        1,
    )


def adder(index, size, live):
    slots = index.shape[1]
    lane = lax.broadcasted_iota(jnp.int32, (size, slots), 1)
    row = lax.broadcasted_iota(jnp.int32, (size, slots), 0)
    return jnp.where((jnp.broadcast_to(index, (size, slots)) == row) & (lane < live), 1.0, 0.0).astype(BF16)


def scatter(products, hot, live):
    slot = lax.broadcasted_iota(jnp.int32, products.shape, 0)
    products = jnp.where(slot < live, products, 0.0)
    high = products.astype(BF16)
    low = (products - high.astype(F32)).astype(BF16)
    both = jnp.dot(hot, jnp.concatenate([high, low], 1), preferred_element_type=F32)
    return both[:, :BS] + both[:, BS:]


def spread(picked):
    row = lax.broadcasted_iota(jnp.int32, (GROUP, BS), 0)
    wide = picked.astype(F32)
    return jnp.concatenate([jnp.where(row == slot, wide, 0.0).astype(BF16) for slot in range(GROUP)], 1)


def multiply(blocks_refs, picked_ref, products_ref):
    base = 0
    for ref in blocks_refs:
        for start in range(0, ref.shape[0], GROUP):
            slots = slice(base + start, base + start + GROUP)
            tile = ref[start : start + GROUP].reshape(GROUP * BS, BS)
            products_ref[slots, :] = jnp.dot(spread(picked_ref[slots, :]), tile, preferred_element_type=F32)
        base += ref.shape[0]


def adjoint_tail(live, data, pick, hot, blocks_refs, keep_ref, send_ref, picked_ref, products_ref):
    picked_ref[...] = jnp.dot(pick, data.astype(BF16), preferred_element_type=F32).astype(BF16)
    multiply(blocks_refs, picked_ref, products_ref)
    partial = scatter(products_ref[...], hot, live)
    keep_ref[...] = partial[:HALF]
    send_ref[:HALF, :] = partial[HALF:].astype(BF16)
    send_ref[HALF:, :] = split_rows(square_sum(data))


def first_adjoint(
    live_ref,
    place_ref,
    own_ref,
    one_ref,
    two_ref,
    three_ref,
    rows_ref,
    cols_ref,
    first_ref,
    second_ref,
    data_ref,
    pick_ref,
    hot_ref,
    keep_ref,
    send_ref,
    picked_ref,
    products_ref,
):
    near, far = square(*NEAR), square(*FAR)
    for step, ref in zip((0, *far), (own_ref, one_ref, two_ref, three_ref)):
        for piece, hop in enumerate((0, *near)):
            at = pl.multiple_of((place_ref[0] ^ step ^ hop) * SHARE, SHARE)
            data_ref[pl.ds(at, SHARE), :] = ref[piece * SHARE : (piece + 1) * SHARE, :]
    live = live_ref[0, 0]
    pick = picker(rows_ref[...], RB)
    hot = adder(cols_ref[...], CB, live)
    pick_ref[...] = pick
    hot_ref[...] = hot
    blocks_refs = (first_ref, second_ref)
    adjoint_tail(live, data_ref[...], pick, hot, blocks_refs, keep_ref, send_ref, picked_ref, products_ref)


def forward_sum(own_ref, one_ref, two_ref, three_ref):
    parts = [ref[...].astype(F32) for ref in (own_ref, one_ref, two_ref, three_ref)]
    return (parts[0] + parts[1]) + (parts[2] + parts[3])


def next_data(own_ref, one_ref, two_ref, three_ref, data_ref, beta2_ref):
    whole = forward_sum(own_ref, one_ref, two_ref, three_ref)
    alpha2 = joined_rows(whole[RB:])
    alpha = jnp.sqrt(alpha2)
    beta = jnp.sqrt(beta2_ref[0:1, :])
    return whole[:RB] / alpha - alpha * (data_ref[...] / beta), alpha2


def second_adjoint(
    live_ref,
    own_ref,
    one_ref,
    two_ref,
    three_ref,
    data_ref,
    beta2_ref,
    pick_ref,
    hot_ref,
    first_ref,
    second_ref,
    next_ref,
    alpha2_ref,
    keep_ref,
    send_ref,
    picked_ref,
    products_ref,
):
    data, alpha2 = next_data(own_ref, one_ref, two_ref, three_ref, data_ref, beta2_ref)
    next_ref[...] = data
    alpha2_ref[...] = jnp.broadcast_to(alpha2, alpha2_ref.shape)
    blocks_refs = (first_ref, second_ref)
    adjoint_tail(
        live_ref[0, 0], data, pick_ref[...], hot_ref[...], blocks_refs, keep_ref, send_ref, picked_ref, products_ref
    )


def chip_sum(keep_ref, send_ref, got_ref, out_ref):
    out_ref[:HALF, :] = (keep_ref[...] + got_ref[:HALF, :].astype(F32)).astype(BF16)
    out_ref[HALF:, :] = split_rows(joined_rows(send_ref[HALF:, :]) + joined_rows(got_ref[HALF:, :]))


def model_sum(own_ref, one_ref, two_ref, three_ref):
    whole = forward_sum(own_ref, one_ref, two_ref, three_ref)
    return whole[:HALF], joined_rows(whole[HALF:])


def model_out(model, beta2, model_ref, send_ref, beta2_ref):
    model_ref[...] = model
    send_ref[:HALF, :] = model.astype(BF16)
    send_ref[HALF:, :] = split_rows(square_sum(model))
    beta2_ref[...] = jnp.broadcast_to(beta2, beta2_ref.shape)


def first_model(own_ref, one_ref, two_ref, three_ref, turned_ref, model_ref, send_ref, beta2_ref):
    total, beta2 = model_sum(own_ref, one_ref, two_ref, three_ref)
    model_out(total / jnp.sqrt(beta2), beta2, model_ref, send_ref, beta2_ref)


def second_model(
    own_ref, one_ref, two_ref, three_ref, last_ref, alpha2_ref, model_ref, send_ref, beta2_ref
):
    total, beta2 = model_sum(own_ref, one_ref, two_ref, three_ref)
    beta = jnp.sqrt(beta2)
    last = last_ref[...] / jnp.sqrt(alpha2_ref[0:1, :])
    model_out(total / beta - beta * last, beta2, model_ref, send_ref, beta2_ref)


def forward(live_ref, own_ref, got_ref, pick_ref, hot_ref, blocks_ref, out_ref, picked_ref, products_ref):
    model = jnp.concatenate([own_ref[:HALF, :], got_ref[:HALF, :]], 0)
    picked_ref[...] = jnp.dot(pick_ref[...], model, preferred_element_type=F32).astype(BF16)
    multiply((blocks_ref,), picked_ref, products_ref)
    out_ref[:RB, :] = scatter(products_ref[...], hot_ref[...], live_ref[0, 0]).astype(BF16)
    out_ref[RB:, :] = split_rows(joined_rows(own_ref[HALF:, :]) + joined_rows(got_ref[HALF:, :]))


def row_sum(own_ref, one_ref, two_ref, three_ref, out_ref):
    whole = forward_sum(own_ref, one_ref, two_ref, three_ref)
    out_ref[:RB, :] = whole[:RB].astype(BF16)
    out_ref[RB:, :] = split_rows(joined_rows(whole[RB:]))


def last_data(own_ref, one_ref, two_ref, three_ref, data_ref, beta2_ref, alpha2_ref, square_ref):
    data, alpha2 = next_data(own_ref, one_ref, two_ref, three_ref, data_ref, beta2_ref)
    alpha2_ref[...] = jnp.broadcast_to(alpha2, alpha2_ref.shape)
    square_ref[...] = jnp.broadcast_to(square_sum(data), square_ref.shape)


def add(own_ref, got_ref, out_ref):
    out_ref[...] = own_ref[...] + got_ref[...]


def finish(
    chip_ref,
    own_ref,
    one_ref,
    two_ref,
    three_ref,
    beta0_ref,
    alpha0_ref,
    beta1_ref,
    alpha1_ref,
    model0_ref,
    model1_ref,
    out_ref,
):
    beta0 = jnp.sqrt(beta0_ref[0:1, :])
    alpha0 = jnp.sqrt(alpha0_ref[0:1, :])
    beta1 = jnp.sqrt(beta1_ref[0:1, :])
    alpha1 = jnp.sqrt(alpha1_ref[0:1, :])
    beta2 = jnp.sqrt(forward_sum(own_ref, one_ref, two_ref, three_ref)[0:1, :])
    chunk = pl.ds(pl.multiple_of(chip_ref[0] * CHUNK, CHUNK), CHUNK)
    model0 = model0_ref[chunk, :] / alpha0
    model1 = model1_ref[chunk, :] / alpha1
    rho1 = jnp.sqrt(alpha0 * alpha0 + beta1 * beta1)
    cosine = alpha0 / rho1
    sine = beta1 / rho1
    theta = sine * alpha1
    rho_bar = -cosine * alpha1
    phi1 = cosine * beta0
    phi_bar = sine * beta0
    search = model1 - theta / rho1 * model0
    rho2 = jnp.sqrt(rho_bar * rho_bar + beta2 * beta2)
    phi2 = rho_bar / rho2 * phi_bar
    out_ref[...] = phi1 / rho1 * model0 + phi2 / rho2 * search


def read(blocks_ref, tile_ref, sems, first):
    pieces = sems.shape[0]
    size = tile_ref.shape[0] // pieces
    return [
        pltpu.make_async_copy(
            blocks_ref.at[pl.ds(first + piece * size, size)],
            tile_ref.at[pl.ds(piece * size, size)],
            sems.at[piece],
        )
        for piece in range(pieces)
    ]


def load_first(
    core_ref,
    chip_ref,
    place_ref,
    live_ref,
    data_ref,
    rows_ref,
    cols_ref,
    blocks_ref,
    data_out,
    rows_out,
    cols_out,
    tile_ref,
    held_ref,
    small_sems,
    sems,
):
    small = [
        pltpu.make_async_copy(cols_ref, held_ref, small_sems.at[0]),
        pltpu.make_async_copy(rows_ref, rows_out, small_sems.at[1]),
        pltpu.make_async_copy(data_ref, data_out, small_sems.at[2]),
    ]
    large = read(blocks_ref, tile_ref, sems, 0)
    for copy in small + large:
        copy.start()
    small[0].wait()
    cols = held_ref[...]
    chunk = jnp.zeros_like(cols)
    for edge in range(CHUNK, CB, CHUNK):
        chunk += jnp.where(cols >= edge, 1, 0)
    half = jnp.where((chunk & 1) == core_ref[0], 0, HALF)
    cols_out[...] = half + (chunk >> 1) * CHUNK + cols - chunk * CHUNK
    for copy in small[1:] + large:
        copy.wait()


def load_second(after_ref, blocks_ref, tile_ref, sems):
    large = read(blocks_ref, tile_ref, sems, tile_ref.shape[0])
    for copy in large:
        copy.start()
    for copy in large:
        copy.wait()


def transpose(live_ref, after_ref, rows_ref, cols_ref, first_ref, second_ref, out_ref, pick_ref, hot_ref):
    pick_ref[...] = picker(cols_ref[...], CB)
    hot_ref[...] = adder(rows_ref[...], RB, live_ref[0, 0])
    half = first_ref.shape[0]
    for slot in range(half):
        out_ref[slot] = jnp.transpose(first_ref[slot])
        out_ref[half + slot] = jnp.transpose(second_ref[slot])


def collect(own_ref, one_ref, two_ref, three_ref, after_ref, out_ref):
    size = own_ref.shape[0]
    for piece, ref in enumerate((own_ref, one_ref, two_ref, three_ref)):
        out_ref[piece * size : (piece + 1) * size, :] = ref[...]


SCALAR = pl.BlockSpec(memory_space=pltpu.SMEM)
VECTOR = pl.BlockSpec(memory_space=pltpu.VMEM)


def call(kernel, outs, vectors, scalars=(), slots=0):
    scratch = [pltpu.VMEM((slots, BS), BF16), pltpu.VMEM((slots, BS), F32)] if slots else []
    return pl.pallas_call(
        kernel,
        out_shape=[jax.ShapeDtypeStruct((rows, *(width or (BS,))), dtype) for rows, dtype, *width in outs],
        in_specs=[SCALAR] * len(scalars) + [VECTOR] * len(vectors),
        out_specs=[VECTOR] * len(outs),
        scratch_shapes=scratch,
        compiler_params=pltpu.CompilerParams(vmem_limit_bytes=16 * 2**20),
        name=kernel.__name__,
    )(*scalars, *vectors)


def body(rhs, blocks, block_rows, block_cols, counts):
    slots = blocks.shape[2]
    group = lax.axis_index("dp")
    core = (group & 1)[None]
    chip = (group >> 1)[None]
    place = lax.axis_index("mp")[None]

    def over_core(x):
        return lax.ppermute(x, "dp", [(i, i ^ 1) for i in range(8)])

    def over_chips(x):
        steps = ((1, 3), (3, 1), (2, 2))
        return [
            lax.ppermute(x, "dp", [(i, (i >> 1 ^ step[i & 1]) * 2 + (i & 1)) for i in range(8)]) for step in steps
        ]

    def over_square(x, others):
        steps = zip(square(*others), square(*others[::-1]))
        return [
            lax.ppermute(
                x, ("dp", "mp"), [(i * 16 + j, i * 16 + (j ^ step[i & 1])) for i in range(8) for j in range(16)]
            )
            for step in steps
        ]

    def over_places(x, others):
        return [lax.ppermute(x, "mp", [(j, j ^ step) for j in range(16)]) for step in square(*others)]

    message = (HALF + EXTRA, BF16)
    scalar = (8, F32)
    model_outs = [(HALF, F32), message, scalar]

    lies = pl.BlockSpec(memory_space=pltpu.HBM)
    inputs = [
        pltpu.with_memory_space_constraint(x, pltpu.HBM) for x in (rhs, block_rows[0], block_cols[0], blocks[0, 0])
    ]
    tile_shape = pltpu.VMEM((slots // 2, BS, BS), BF16)
    params = pltpu.CompilerParams(vmem_limit_bytes=16 * 2**20)
    cost = pl.CostEstimate(flops=0, bytes_accessed=slots * BS * BS * 2, transcendentals=0)
    data, rows, cols, first = pl.pallas_call(
        load_first,
        out_shape=[
            jax.ShapeDtypeStruct(rhs.shape, F32),
            jax.ShapeDtypeStruct((1, slots), jnp.int32),
            jax.ShapeDtypeStruct((1, slots), jnp.int32),
            tile_shape,
        ],
        in_specs=[SCALAR] * 4 + [lies] * 4,
        out_specs=[VECTOR] * 4,
        scratch_shapes=[
            pltpu.VMEM((1, slots), jnp.int32),
            pltpu.SemaphoreType.DMA((3,)),
            pltpu.SemaphoreType.DMA((LOADS,)),
        ],
        compiler_params=params,
        cost_estimate=cost,
        name="load_first",
    )(core, chip, place, counts, *inputs)
    first = pltpu.with_memory_space_constraint(first, pltpu.VMEM)
    (quarter,) = call(collect, [(4 * SHARE, F32)], [data, *over_places(rhs, NEAR), first])
    second = pl.pallas_call(
        load_second,
        out_shape=tile_shape,
        in_specs=[VECTOR, lies],
        out_specs=VECTOR,
        scratch_shapes=[pltpu.SemaphoreType.DMA((LOADS,))],
        compiler_params=params,
        cost_estimate=cost,
        name="load_second",
    )(quarter, inputs[-1])
    second = pltpu.with_memory_space_constraint(second, pltpu.VMEM)

    def forward_whole(own):
        (part,) = call(forward, [(RB + EXTRA, BF16)], [own, over_core(own), pick_cols, add_rows, turned], [counts], slots)
        (part,) = call(row_sum, [(RB + EXTRA, BF16)], [part, *over_square(part, NEAR)])
        return [part, *over_square(part, FAR)]

    def chips_whole(part):
        return [part, *over_chips(part)]

    data0, pick_rows, add_cols, keep, send = call(
        first_adjoint,
        [(RB, F32), (slots, BF16, RB), (CB, BF16, slots), (HALF, F32), message],
        [quarter, *over_places(quarter, FAR), rows, cols, first, second],
        [counts, place],
        slots,
    )
    (part,) = call(chip_sum, [message], [keep, send, over_core(send)])
    turned, pick_cols, add_rows = pl.pallas_call(
        transpose,
        out_shape=[
            pltpu.VMEM((slots, BS, BS), BF16),
            jax.ShapeDtypeStruct((slots, CB), BF16),
            jax.ShapeDtypeStruct((RB, slots), BF16),
        ],
        in_specs=[SCALAR] + [VECTOR] * 5,
        out_specs=[VECTOR] * 3,
        compiler_params=params,
        cost_estimate=cost,
        name="transpose",
    )(counts, part, rows, cols, first, second)
    turned = pltpu.with_memory_space_constraint(turned, pltpu.VMEM)
    model0, own, beta0 = call(first_model, model_outs, [*chips_whole(part), turned])
    data1, alpha0, keep, send = call(
        second_adjoint,
        [(RB, F32), scalar, (HALF, F32), message],
        [*forward_whole(own), data0, beta0, pick_rows, add_cols, first, second],
        [counts],
        slots,
    )
    (part,) = call(chip_sum, [message], [keep, send, over_core(send)])
    model1, own, beta1 = call(second_model, model_outs, [*chips_whole(part), model0, alpha0])
    alpha1, total = call(last_data, [scalar, scalar], [*forward_whole(own), data1, beta1])
    (total,) = call(add, [scalar], [total, over_core(total)])
    (out,) = call(
        finish,
        [(CHUNK, F32)],
        [total, *over_chips(total), beta0, alpha0, beta1, alpha1, model0, model1],
        [chip],
    )
    return out


def solution(mesh):
    placed = (
        P(("dp", "mp"), None),
        P("dp", "mp", None, None, None),
        P("dp", "mp", None),
        P("dp", "mp", None),
        P("dp", "mp"),
    )
    return jax.shard_map(
        body, mesh=mesh, in_specs=placed, out_specs=P(("mp", "dp"), None), check_vma=False
    )
```

```python
import functools

import jax
import jax.numpy as jnp
from jax import lax
from jax.experimental import pallas as pl
from jax.experimental.pallas import tpu as pltpu
from jax.sharding import PartitionSpec as P

BS = 128
RB = 512
CB = 768
HALF = CB // 2
CHUNK = 96
GROUP = 16
EXTRA = 16
LOADS = 8
SHARE = 32
NEAR = (1, 3)
FAR = (3, 1)
F32 = jnp.float32
BF16 = jnp.bfloat16


def square(other_x, other_y):
    return other_y, 4 * other_x, 4 * other_x + other_y


def split_rows(value):
    row = lax.broadcasted_iota(jnp.int32, (EXTRA, BS), 0)
    value = jnp.broadcast_to(value, (EXTRA, BS))
    high = value.astype(BF16).astype(F32)
    rest = value - high
    middle = rest.astype(BF16).astype(F32)
    low = rest - middle
    zero = jnp.zeros_like(value)
    return jnp.where(row == 0, high, jnp.where(row == 1, middle, jnp.where(row == 2, low, zero))).astype(BF16)


def joined_rows(rows):
    return jnp.sum(rows.astype(F32), axis=0, keepdims=True)


def square_sum(x):
    return jnp.sum(jnp.sum(x * x, axis=0, keepdims=True), axis=1, keepdims=True)


def column(index):
    pieces = []
    for start in range(0, index.shape[1], BS):
        row = jnp.broadcast_to(index[:, start : start + BS].astype(F32), (BS, BS))
        pieces.append(jnp.transpose(row))
    return jnp.concatenate(pieces, 0)


def picker(index, size):
    at = column(index)
    lane = lax.broadcasted_iota(jnp.int32, at.shape, 1)
    return jnp.concatenate(
        [
            jnp.where(at == (lane + start).astype(F32), 1.0, 0.0).astype(BF16)
            for start in range(0, size, BS)
        ],
        1,
    )


def adder(index, size, live):
    slots = index.shape[1]
    lane = lax.broadcasted_iota(jnp.int32, (size, slots), 1)
    row = lax.broadcasted_iota(jnp.int32, (size, slots), 0)
    return jnp.where((jnp.broadcast_to(index, (size, slots)) == row) & (lane < live), 1.0, 0.0).astype(BF16)


def gather(pick_ref, source, picked_ref):
    for start in reversed(range(0, picked_ref.shape[0], BS)):
        piece = jnp.dot(pick_ref[start : start + BS, :], source, preferred_element_type=F32)
        picked_ref[start : start + BS, :] = piece.astype(BF16)


def scatter(products_ref, hot_ref, live):
    slots = products_ref.shape[0]
    total = 0.0
    for start in range(0, slots, 2 * BS):
        piece = slice(start, min(start + 2 * BS, slots))
        products = products_ref[piece, :]
        slot = lax.broadcasted_iota(jnp.int32, products.shape, 0) + start
        products = jnp.where(slot < live, products, 0.0)
        high = products.astype(BF16)
        low = (products - high.astype(F32)).astype(BF16)
        total += jnp.dot(hot_ref[:, piece], jnp.concatenate([high, low], 1), preferred_element_type=F32)
    return total[:, :BS] + total[:, BS:]


def spread(picked):
    row = lax.broadcasted_iota(jnp.int32, (GROUP, BS), 0)
    wide = picked.astype(F32)
    return jnp.concatenate([jnp.where(row == slot, wide, 0.0).astype(BF16) for slot in range(GROUP)], 1)


def multiply(blocks_refs, picked_ref, products_ref):
    def block(slot, size):
        for ref in blocks_refs:
            if slot < ref.shape[0]:
                return ref[slot : slot + size]
            slot -= ref.shape[0]

    slots = picked_ref.shape[0]
    singles = slots // 4
    groups = (slots - singles) // GROUP
    first = groups * GROUP
    turned = []
    for start in range(first, slots, BS):
        rows = picked_ref[start : min(start + BS, slots), :].astype(F32)
        if rows.shape[0] < BS:
            rows = jnp.concatenate([rows, jnp.zeros((BS - rows.shape[0], BS), F32)], 0)
        turned.append(jnp.transpose(rows))
    for group in range(groups):
        for single in range(singles * group // groups, singles * (group + 1) // groups):
            weights = jnp.broadcast_to(turned[single // BS][:, single % BS : single % BS + 1], (BS, BS))
            product = block(first + single, 1)[0].astype(F32) * weights
            products_ref[first + single : first + single + 1, :] = jnp.sum(product, axis=0, keepdims=True)
        start = group * GROUP
        tile = block(start, GROUP).reshape(GROUP * BS, BS)
        products_ref[start : start + GROUP, :] = jnp.dot(
            spread(picked_ref[start : start + GROUP, :]), tile, preferred_element_type=F32
        )


def adjoint_tail(live, data, pick_ref, hot_ref, blocks_refs, keep_ref, send_ref, picked_ref, products_ref):
    gather(pick_ref, data.astype(BF16), picked_ref)
    multiply(blocks_refs, picked_ref, products_ref)
    partial = scatter(products_ref, hot_ref, live)
    keep_ref[...] = partial[:HALF]
    send_ref[:HALF, :] = partial[HALF:].astype(BF16)
    send_ref[HALF:, :] = split_rows(square_sum(data))


def first_adjoint(
    live_ref,
    place_ref,
    own_ref,
    one_ref,
    two_ref,
    three_ref,
    rows_ref,
    cols_ref,
    first_ref,
    second_ref,
    data_ref,
    pick_ref,
    hot_ref,
    keep_ref,
    send_ref,
    picked_ref,
    products_ref,
):
    near, far = square(*NEAR), square(*FAR)
    for step, ref in zip((0, *far), (own_ref, one_ref, two_ref, three_ref)):
        for piece, hop in enumerate((0, *near)):
            at = pl.multiple_of((place_ref[0] ^ step ^ hop) * SHARE, SHARE)
            data_ref[pl.ds(at, SHARE), :] = ref[piece * SHARE : (piece + 1) * SHARE, :]
    live = live_ref[0, 0]
    pick_ref[...] = picker(rows_ref[...], RB)
    hot_ref[...] = adder(cols_ref[...], CB, live)
    blocks_refs = (first_ref, second_ref)
    adjoint_tail(live, data_ref[...], pick_ref, hot_ref, blocks_refs, keep_ref, send_ref, picked_ref, products_ref)


def forward_sum(own_ref, one_ref, two_ref, three_ref):
    parts = [ref[...].astype(F32) for ref in (own_ref, one_ref, two_ref, three_ref)]
    return (parts[0] + parts[1]) + (parts[2] + parts[3])


def next_data(own_ref, one_ref, two_ref, three_ref, data_ref, beta2_ref):
    whole = forward_sum(own_ref, one_ref, two_ref, three_ref)
    alpha2 = joined_rows(whole[RB:])
    alpha = jnp.sqrt(alpha2)
    beta = jnp.sqrt(beta2_ref[0:1, :])
    return whole[:RB] * (1.0 / alpha) - data_ref[...] * (alpha / beta), alpha2


def second_adjoint(
    live_ref,
    own_ref,
    one_ref,
    two_ref,
    three_ref,
    data_ref,
    beta2_ref,
    pick_ref,
    hot_ref,
    first_ref,
    second_ref,
    next_ref,
    alpha2_ref,
    keep_ref,
    send_ref,
    picked_ref,
    products_ref,
):
    data, alpha2 = next_data(own_ref, one_ref, two_ref, three_ref, data_ref, beta2_ref)
    next_ref[...] = data
    alpha2_ref[...] = jnp.broadcast_to(alpha2, alpha2_ref.shape)
    blocks_refs = (first_ref, second_ref)
    adjoint_tail(
        live_ref[0, 0], data, pick_ref, hot_ref, blocks_refs, keep_ref, send_ref, picked_ref, products_ref
    )


def chip_sum(keep_ref, send_ref, got_ref, out_ref):
    out_ref[:HALF, :] = (keep_ref[...] + got_ref[:HALF, :].astype(F32)).astype(BF16)
    out_ref[HALF:, :] = split_rows(joined_rows(send_ref[HALF:, :]) + joined_rows(got_ref[HALF:, :]))


def model_sum(own_ref, one_ref, two_ref, three_ref):
    whole = forward_sum(own_ref, one_ref, two_ref, three_ref)
    return whole[:HALF], joined_rows(whole[HALF:])


def model_out(model, beta2, model_ref, send_ref, beta2_ref):
    model_ref[...] = model
    send_ref[:HALF, :] = model.astype(BF16)
    send_ref[HALF:, :] = split_rows(square_sum(model))
    beta2_ref[...] = jnp.broadcast_to(beta2, beta2_ref.shape)


def first_model(own_ref, one_ref, two_ref, three_ref, turned_ref, model_ref, send_ref, beta2_ref):
    total, beta2 = model_sum(own_ref, one_ref, two_ref, three_ref)
    model_out(total * (1.0 / jnp.sqrt(beta2)), beta2, model_ref, send_ref, beta2_ref)


def second_model(
    own_ref, one_ref, two_ref, three_ref, last_ref, alpha2_ref, model_ref, send_ref, beta2_ref
):
    total, beta2 = model_sum(own_ref, one_ref, two_ref, three_ref)
    beta = jnp.sqrt(beta2)
    alpha = jnp.sqrt(alpha2_ref[0:1, :])
    model_out(total * (1.0 / beta) - last_ref[...] * (beta / alpha), beta2, model_ref, send_ref, beta2_ref)


def forward(live_ref, own_ref, got_ref, pick_ref, hot_ref, blocks_ref, out_ref, picked_ref, products_ref):
    model = jnp.concatenate([own_ref[:HALF, :], got_ref[:HALF, :]], 0)
    gather(pick_ref, model, picked_ref)
    multiply((blocks_ref,), picked_ref, products_ref)
    out_ref[:RB, :] = scatter(products_ref, hot_ref, live_ref[0, 0]).astype(BF16)
    out_ref[RB:, :] = split_rows(joined_rows(own_ref[HALF:, :]) + joined_rows(got_ref[HALF:, :]))


def row_sum(own_ref, one_ref, two_ref, three_ref, out_ref):
    whole = forward_sum(own_ref, one_ref, two_ref, three_ref)
    out_ref[:RB, :] = whole[:RB].astype(BF16)
    out_ref[RB:, :] = split_rows(joined_rows(whole[RB:]))


def last_data(own_ref, one_ref, two_ref, three_ref, data_ref, beta2_ref, alpha2_ref, square_ref):
    data, alpha2 = next_data(own_ref, one_ref, two_ref, three_ref, data_ref, beta2_ref)
    alpha2_ref[...] = jnp.broadcast_to(alpha2, alpha2_ref.shape)
    square_ref[...] = jnp.broadcast_to(square_sum(data), square_ref.shape)


def add(own_ref, got_ref, out_ref):
    out_ref[...] = own_ref[...] + got_ref[...]


def finish(
    chip_ref,
    own_ref,
    one_ref,
    two_ref,
    three_ref,
    beta0_ref,
    alpha0_ref,
    beta1_ref,
    alpha1_ref,
    model0_ref,
    model1_ref,
    out_ref,
):
    beta0 = jnp.sqrt(beta0_ref[0:1, :])
    alpha0 = jnp.sqrt(alpha0_ref[0:1, :])
    beta1 = jnp.sqrt(beta1_ref[0:1, :])
    alpha1 = jnp.sqrt(alpha1_ref[0:1, :])
    beta2 = jnp.sqrt(forward_sum(own_ref, one_ref, two_ref, three_ref)[0:1, :])
    chunk = pl.ds(pl.multiple_of(chip_ref[0] * CHUNK, CHUNK), CHUNK)
    model0 = model0_ref[chunk, :] / alpha0
    model1 = model1_ref[chunk, :] / alpha1
    rho1 = jnp.sqrt(alpha0 * alpha0 + beta1 * beta1)
    cosine = alpha0 / rho1
    sine = beta1 / rho1
    theta = sine * alpha1
    rho_bar = -cosine * alpha1
    phi1 = cosine * beta0
    phi_bar = sine * beta0
    search = model1 - theta / rho1 * model0
    rho2 = jnp.sqrt(rho_bar * rho_bar + beta2 * beta2)
    phi2 = rho_bar / rho2 * phi_bar
    out_ref[...] = phi1 / rho1 * model0 + phi2 / rho2 * search


def read(blocks_ref, tile_ref, sems, first):
    pieces = sems.shape[0]
    size = tile_ref.shape[0] // pieces
    return [
        pltpu.make_async_copy(
            blocks_ref.at[pl.ds(first + piece * size, size)],
            tile_ref.at[pl.ds(piece * size, size)],
            sems.at[piece],
        )
        for piece in range(pieces)
    ]


def load_first(
    core_ref,
    chip_ref,
    place_ref,
    live_ref,
    data_ref,
    rows_ref,
    cols_ref,
    blocks_ref,
    data_out,
    rows_out,
    cols_out,
    tile_ref,
    held_ref,
    small_sems,
    sems,
):
    small = [
        pltpu.make_async_copy(cols_ref, held_ref, small_sems.at[0]),
        pltpu.make_async_copy(rows_ref, rows_out, small_sems.at[1]),
        pltpu.make_async_copy(data_ref, data_out, small_sems.at[2]),
    ]
    large = read(blocks_ref, tile_ref, sems, 0)
    for copy in small + large:
        copy.start()
    small[0].wait()
    cols = held_ref[...]
    chunk = jnp.zeros_like(cols)
    for edge in range(CHUNK, CB, CHUNK):
        chunk += jnp.where(cols >= edge, 1, 0)
    half = jnp.where((chunk & 1) == core_ref[0], 0, HALF)
    cols_out[...] = half + (chunk >> 1) * CHUNK + cols - chunk * CHUNK
    for copy in small[1:] + large:
        copy.wait()


def load_second(after_ref, blocks_ref, tile_ref, sems):
    large = read(blocks_ref, tile_ref, sems, blocks_ref.shape[0] - tile_ref.shape[0])
    for copy in large:
        copy.start()
    for copy in large:
        copy.wait()


def transpose(live_ref, after_ref, rows_ref, cols_ref, first_ref, second_ref, out_ref, pick_ref, hot_ref):
    pick_ref[...] = picker(cols_ref[...], CB)
    hot_ref[...] = adder(rows_ref[...], RB, live_ref[0, 0])
    base = 0
    for ref in (first_ref, second_ref):
        for slot in range(ref.shape[0]):
            out_ref[base + slot] = jnp.transpose(ref[slot])
        base += ref.shape[0]


def collect(own_ref, one_ref, two_ref, three_ref, after_ref, out_ref):
    size = own_ref.shape[0]
    for piece, ref in enumerate((own_ref, one_ref, two_ref, three_ref)):
        out_ref[piece * size : (piece + 1) * size, :] = ref[...]


SCALAR = pl.BlockSpec(memory_space=pltpu.SMEM)
VECTOR = pl.BlockSpec(memory_space=pltpu.VMEM)


def call(kernel, outs, vectors, scalars=(), slots=0):
    scratch = [pltpu.VMEM((slots, BS), BF16), pltpu.VMEM((slots, BS), F32)] if slots else []
    return pl.pallas_call(
        kernel,
        out_shape=[jax.ShapeDtypeStruct((rows, *(width or (BS,))), dtype) for rows, dtype, *width in outs],
        in_specs=[SCALAR] * len(scalars) + [VECTOR] * len(vectors),
        out_specs=[VECTOR] * len(outs),
        scratch_shapes=scratch,
        compiler_params=pltpu.CompilerParams(vmem_limit_bytes=16 * 2**20),
        name=kernel.__name__,
    )(*scalars, *vectors)


def body(rhs, blocks, block_rows, block_cols, counts):
    slots = blocks.shape[2]
    group = lax.axis_index("dp")
    core = (group & 1)[None]
    chip = (group >> 1)[None]
    place = lax.axis_index("mp")[None]

    def over_core(x):
        return lax.ppermute(x, "dp", [(i, i ^ 1) for i in range(8)])

    def over_chips(x):
        steps = ((1, 3), (3, 1), (2, 2))
        return [
            lax.ppermute(x, "dp", [(i, (i >> 1 ^ step[i & 1]) * 2 + (i & 1)) for i in range(8)]) for step in steps
        ]

    def over_square(x, others):
        steps = zip(square(*others), square(*others[::-1]))
        return [
            lax.ppermute(
                x, ("dp", "mp"), [(i * 16 + j, i * 16 + (j ^ step[i & 1])) for i in range(8) for j in range(16)]
            )
            for step in steps
        ]

    def over_places(x, others):
        return [lax.ppermute(x, "mp", [(j, j ^ step) for j in range(16)]) for step in square(*others)]

    message = (HALF + EXTRA, BF16)
    scalar = (8, F32)
    model_outs = [(HALF, F32), message, scalar]

    lies = pl.BlockSpec(memory_space=pltpu.HBM)
    inputs = [
        pltpu.with_memory_space_constraint(x, pltpu.HBM) for x in (rhs, block_rows[0], block_cols[0], blocks[0, 0])
    ]
    early = slots * 3 // 8
    first_shape = pltpu.VMEM((early, BS, BS), BF16)
    second_shape = pltpu.VMEM((slots - early, BS, BS), BF16)
    params = pltpu.CompilerParams(vmem_limit_bytes=16 * 2**20)
    cost = pl.CostEstimate(flops=0, bytes_accessed=slots * BS * BS * 2, transcendentals=0)
    data, rows, cols, first = pl.pallas_call(
        load_first,
        out_shape=[
            jax.ShapeDtypeStruct(rhs.shape, F32),
            jax.ShapeDtypeStruct((1, slots), jnp.int32),
            jax.ShapeDtypeStruct((1, slots), jnp.int32),
            first_shape,
        ],
        in_specs=[SCALAR] * 4 + [lies] * 4,
        out_specs=[VECTOR] * 4,
        scratch_shapes=[
            pltpu.VMEM((1, slots), jnp.int32),
            pltpu.SemaphoreType.DMA((3,)),
            pltpu.SemaphoreType.DMA((LOADS,)),
        ],
        compiler_params=params,
        cost_estimate=cost,
        name="load_first",
    )(core, chip, place, counts, *inputs)
    first = pltpu.with_memory_space_constraint(first, pltpu.VMEM)
    (quarter,) = call(collect, [(4 * SHARE, F32)], [data, *over_places(rhs, NEAR), first])
    second = pl.pallas_call(
        load_second,
        out_shape=second_shape,
        in_specs=[VECTOR, lies],
        out_specs=VECTOR,
        scratch_shapes=[pltpu.SemaphoreType.DMA((LOADS,))],
        compiler_params=params,
        cost_estimate=cost,
        name="load_second",
    )(quarter, inputs[-1])
    second = pltpu.with_memory_space_constraint(second, pltpu.VMEM)

    def forward_whole(own):
        (part,) = call(forward, [(RB + EXTRA, BF16)], [own, over_core(own), pick_cols, add_rows, turned], [counts], slots)
        (part,) = call(row_sum, [(RB + EXTRA, BF16)], [part, *over_square(part, NEAR)])
        return [part, *over_square(part, FAR)]

    def chips_whole(part):
        return [part, *over_chips(part)]

    data0, pick_rows, add_cols, keep, send = call(
        first_adjoint,
        [(RB, F32), (slots, BF16, RB), (CB, BF16, slots), (HALF, F32), message],
        [quarter, *over_places(quarter, FAR), rows, cols, first, second],
        [counts, place],
        slots,
    )
    (part,) = call(chip_sum, [message], [keep, send, over_core(send)])
    turned, pick_cols, add_rows = pl.pallas_call(
        transpose,
        out_shape=[
            pltpu.VMEM((slots, BS, BS), BF16),
            jax.ShapeDtypeStruct((slots, CB), BF16),
            jax.ShapeDtypeStruct((RB, slots), BF16),
        ],
        in_specs=[SCALAR] + [VECTOR] * 5,
        out_specs=[VECTOR] * 3,
        compiler_params=params,
        cost_estimate=cost,
        name="transpose",
    )(counts, part, rows, cols, first, second)
    turned = pltpu.with_memory_space_constraint(turned, pltpu.VMEM)
    model0, own, beta0 = call(first_model, model_outs, [*chips_whole(part), turned])
    data1, alpha0, keep, send = call(
        second_adjoint,
        [(RB, F32), scalar, (HALF, F32), message],
        [*forward_whole(own), data0, beta0, pick_rows, add_cols, first, second],
        [counts],
        slots,
    )
    (part,) = call(chip_sum, [message], [keep, send, over_core(send)])
    model1, own, beta1 = call(second_model, model_outs, [*chips_whole(part), model0, alpha0])
    alpha1, total = call(last_data, [scalar, scalar], [*forward_whole(own), data1, beta1])
    (total,) = call(add, [scalar], [total, over_core(total)])
    (out,) = call(
        finish,
        [(CHUNK, F32)],
        [total, *over_chips(total), beta0, alpha0, beta1, alpha1, model0, model1],
        [chip],
    )
    return out


def solution(mesh):
    placed = (
        P(("dp", "mp"), None),
        P("dp", "mp", None, None, None),
        P("dp", "mp", None),
        P("dp", "mp", None),
        P("dp", "mp"),
    )
    return jax.shard_map(
        body, mesh=mesh, in_specs=placed, out_specs=P(("mp", "dp"), None), check_vma=False
    )
```

```python
import functools

import jax
import jax.numpy as jnp
from jax import lax
from jax.experimental import pallas as pl
from jax.experimental.pallas import tpu as pltpu
from jax.sharding import PartitionSpec as P

BS = 128
RB = 512
CB = 768
HALF = CB // 2
CHUNK = 96
GROUP = 16
EXTRA = 16
LOADS = 8
SHARE = 32
NEAR = (1, 3)
FAR = (3, 1)
F32 = jnp.float32
BF16 = jnp.bfloat16


def square(other_x, other_y):
    return other_y, 4 * other_x, 4 * other_x + other_y


def split_rows(value):
    row = lax.broadcasted_iota(jnp.int32, (EXTRA, BS), 0)
    value = jnp.broadcast_to(value, (EXTRA, BS))
    high = value.astype(BF16).astype(F32)
    rest = value - high
    middle = rest.astype(BF16).astype(F32)
    low = rest - middle
    zero = jnp.zeros_like(value)
    return jnp.where(row == 0, high, jnp.where(row == 1, middle, jnp.where(row == 2, low, zero))).astype(BF16)


def joined_rows(rows):
    return jnp.sum(rows.astype(F32), axis=0, keepdims=True)


def square_sum(x):
    return jnp.sum(jnp.sum(x * x, axis=0, keepdims=True), axis=1, keepdims=True)


def column(index):
    pieces = []
    for start in range(0, index.shape[1], BS):
        row = jnp.broadcast_to(index[:, start : start + BS].astype(F32), (BS, BS))
        pieces.append(jnp.transpose(row))
    return jnp.concatenate(pieces, 0)


def picker(index, size, live):
    at = column(index)
    lane = lax.broadcasted_iota(jnp.int32, at.shape, 1)
    slot = lax.broadcasted_iota(jnp.int32, at.shape, 0)
    return jnp.concatenate(
        [
            jnp.where((at == (lane + start).astype(F32)) & (slot < live), 1.0, 0.0).astype(BF16)
            for start in range(0, size, BS)
        ],
        1,
    )


def adder(index, size, live):
    slots = index.shape[1]
    lane = lax.broadcasted_iota(jnp.int32, (size, slots), 1)
    row = lax.broadcasted_iota(jnp.int32, (size, slots), 0)
    return jnp.where((jnp.broadcast_to(index, (size, slots)) == row) & (lane < live), 1.0, 0.0).astype(BF16)


def gather(pick_ref, source, picked_ref):
    for start in range(0, picked_ref.shape[0], BS):
        piece = jnp.dot(pick_ref[start : start + BS, :], source, preferred_element_type=F32)
        picked_ref[start : start + BS, :] = piece.astype(BF16)


def scatter(products_ref, hot_ref):
    slots = products_ref.shape[0]
    total = 0.0
    for start in range(0, slots, 2 * BS):
        piece = slice(start, min(start + 2 * BS, slots))
        products = products_ref[piece, :]
        high = products.astype(BF16)
        low = (products - high.astype(F32)).astype(BF16)
        total += jnp.dot(hot_ref[:, piece], jnp.concatenate([high, low], 1), preferred_element_type=F32)
    return total[:, :BS] + total[:, BS:]


def spread(picked):
    row = lax.broadcasted_iota(jnp.int32, (GROUP, BS), 0)
    wide = picked.astype(F32)
    return jnp.concatenate([jnp.where(row == slot, wide, 0.0).astype(BF16) for slot in range(GROUP)], 1)


def multiply(blocks_refs, picked_ref, products_ref):
    def block(slot, size):
        for ref in blocks_refs:
            if slot < ref.shape[0]:
                return ref[slot : slot + size]
            slot -= ref.shape[0]

    slots = picked_ref.shape[0]
    singles = slots // 4
    groups = (slots - singles) // GROUP
    turned = []
    for start in range(0, singles, BS):
        rows = picked_ref[start : min(start + BS, singles), :].astype(F32)
        if rows.shape[0] < BS:
            rows = jnp.concatenate([rows, jnp.zeros((BS - rows.shape[0], BS), F32)], 0)
        turned.append(jnp.transpose(rows))
    for group in range(groups):
        start = singles + group * GROUP
        for single in range(singles * group // groups, singles * (group + 1) // groups):
            weights = jnp.broadcast_to(turned[single // BS][:, single % BS : single % BS + 1], (BS, BS))
            product = block(single, 1)[0].astype(F32) * weights
            products_ref[single : single + 1, :] = jnp.sum(product, axis=0, keepdims=True)
        tile = block(start, GROUP).reshape(GROUP * BS, BS)
        products_ref[start : start + GROUP, :] = jnp.dot(
            spread(picked_ref[start : start + GROUP, :]), tile, preferred_element_type=F32
        )


def adjoint_tail(data, pick_ref, hot_ref, blocks_refs, keep_ref, send_ref, picked_ref, products_ref):
    gather(pick_ref, data.astype(BF16), picked_ref)
    multiply(blocks_refs, picked_ref, products_ref)
    partial = scatter(products_ref, hot_ref)
    keep_ref[...] = partial[:HALF]
    send_ref[:HALF, :] = partial[HALF:].astype(BF16)
    send_ref[HALF:, :] = split_rows(square_sum(data))


def first_adjoint(
    live_ref,
    own_ref,
    one_ref,
    two_ref,
    three_ref,
    rows_ref,
    cols_ref,
    first_ref,
    second_ref,
    data_ref,
    pick_ref,
    hot_ref,
    keep_ref,
    send_ref,
    picked_ref,
    products_ref,
):
    near, far = square(*NEAR), square(*FAR)
    place = lax.axis_index("mp")
    for step, ref in zip((0, *far), (own_ref, one_ref, two_ref, three_ref)):
        for piece, hop in enumerate((0, *near)):
            at = pl.multiple_of((place ^ step ^ hop) * SHARE, SHARE)
            data_ref[pl.ds(at, SHARE), :] = ref[piece * SHARE : (piece + 1) * SHARE, :]
    live = live_ref[0, 0]
    pick_ref[...] = picker(rows_ref[...], RB, live)
    hot_ref[...] = adder(cols_ref[...], CB, live)
    blocks_refs = (first_ref, second_ref)
    adjoint_tail(data_ref[...], pick_ref, hot_ref, blocks_refs, keep_ref, send_ref, picked_ref, products_ref)


def forward_sum(own_ref, one_ref, two_ref, three_ref):
    parts = [ref[...].astype(F32) for ref in (own_ref, one_ref, two_ref, three_ref)]
    return (parts[0] + parts[1]) + (parts[2] + parts[3])


def next_data(own_ref, one_ref, two_ref, three_ref, data_ref, beta2_ref):
    whole = forward_sum(own_ref, one_ref, two_ref, three_ref)
    alpha2 = joined_rows(whole[RB:])
    alpha = jnp.sqrt(alpha2)
    beta = jnp.sqrt(beta2_ref[0:1, :])
    return whole[:RB] * (1.0 / alpha) - data_ref[...] * (alpha / beta), alpha2


def second_adjoint(
    own_ref,
    one_ref,
    two_ref,
    three_ref,
    data_ref,
    beta2_ref,
    pick_ref,
    hot_ref,
    first_ref,
    second_ref,
    next_ref,
    alpha2_ref,
    keep_ref,
    send_ref,
    picked_ref,
    products_ref,
):
    data, alpha2 = next_data(own_ref, one_ref, two_ref, three_ref, data_ref, beta2_ref)
    next_ref[...] = data
    alpha2_ref[...] = jnp.broadcast_to(alpha2, alpha2_ref.shape)
    blocks_refs = (first_ref, second_ref)
    adjoint_tail(
        data, pick_ref, hot_ref, blocks_refs, keep_ref, send_ref, picked_ref, products_ref
    )


def chip_sum(keep_ref, send_ref, got_ref, out_ref):
    out_ref[:HALF, :] = (keep_ref[...] + got_ref[:HALF, :].astype(F32)).astype(BF16)
    out_ref[HALF:, :] = split_rows(joined_rows(send_ref[HALF:, :]) + joined_rows(got_ref[HALF:, :]))


def model_sum(own_ref, one_ref, two_ref, three_ref):
    whole = forward_sum(own_ref, one_ref, two_ref, three_ref)
    return whole[:HALF], joined_rows(whole[HALF:])


def model_out(model, beta2, model_ref, send_ref, beta2_ref):
    model_ref[...] = model
    send_ref[:HALF, :] = model.astype(BF16)
    send_ref[HALF:, :] = split_rows(square_sum(model))
    beta2_ref[...] = jnp.broadcast_to(beta2, beta2_ref.shape)


def first_model(own_ref, one_ref, two_ref, three_ref, turned_ref, model_ref, send_ref, beta2_ref):
    total, beta2 = model_sum(own_ref, one_ref, two_ref, three_ref)
    model_out(total * (1.0 / jnp.sqrt(beta2)), beta2, model_ref, send_ref, beta2_ref)


def second_model(
    own_ref, one_ref, two_ref, three_ref, last_ref, alpha2_ref, model_ref, send_ref, beta2_ref
):
    total, beta2 = model_sum(own_ref, one_ref, two_ref, three_ref)
    beta = jnp.sqrt(beta2)
    alpha = jnp.sqrt(alpha2_ref[0:1, :])
    model_out(total * (1.0 / beta) - last_ref[...] * (beta / alpha), beta2, model_ref, send_ref, beta2_ref)


def forward(own_ref, got_ref, pick_ref, hot_ref, blocks_ref, out_ref, picked_ref, products_ref):
    model = jnp.concatenate([own_ref[:HALF, :], got_ref[:HALF, :]], 0)
    gather(pick_ref, model, picked_ref)
    multiply((blocks_ref,), picked_ref, products_ref)
    out_ref[:RB, :] = scatter(products_ref, hot_ref).astype(BF16)
    out_ref[RB:, :] = split_rows(joined_rows(own_ref[HALF:, :]) + joined_rows(got_ref[HALF:, :]))


def row_sum(own_ref, one_ref, two_ref, three_ref, out_ref):
    whole = forward_sum(own_ref, one_ref, two_ref, three_ref)
    out_ref[:RB, :] = whole[:RB].astype(BF16)
    out_ref[RB:, :] = split_rows(joined_rows(whole[RB:]))


def last_data(own_ref, one_ref, two_ref, three_ref, data_ref, beta2_ref, alpha2_ref, square_ref):
    data, alpha2 = next_data(own_ref, one_ref, two_ref, three_ref, data_ref, beta2_ref)
    alpha2_ref[...] = jnp.broadcast_to(alpha2, alpha2_ref.shape)
    square_ref[...] = jnp.broadcast_to(square_sum(data), square_ref.shape)


def add(own_ref, got_ref, out_ref):
    out_ref[...] = own_ref[...] + got_ref[...]


def finish(
    own_ref,
    one_ref,
    two_ref,
    three_ref,
    beta0_ref,
    alpha0_ref,
    beta1_ref,
    alpha1_ref,
    model0_ref,
    model1_ref,
    out_ref,
):
    beta0 = jnp.sqrt(beta0_ref[0:1, :])
    alpha0 = jnp.sqrt(alpha0_ref[0:1, :])
    beta1 = jnp.sqrt(beta1_ref[0:1, :])
    alpha1 = jnp.sqrt(alpha1_ref[0:1, :])
    beta2 = jnp.sqrt(forward_sum(own_ref, one_ref, two_ref, three_ref)[0:1, :])
    chunk = pl.ds(pl.multiple_of((lax.axis_index("dp") >> 1) * CHUNK, CHUNK), CHUNK)
    model0 = model0_ref[chunk, :] / alpha0
    model1 = model1_ref[chunk, :] / alpha1
    rho1 = jnp.sqrt(alpha0 * alpha0 + beta1 * beta1)
    cosine = alpha0 / rho1
    sine = beta1 / rho1
    theta = sine * alpha1
    rho_bar = -cosine * alpha1
    phi1 = cosine * beta0
    phi_bar = sine * beta0
    search = model1 - theta / rho1 * model0
    rho2 = jnp.sqrt(rho_bar * rho_bar + beta2 * beta2)
    phi2 = rho_bar / rho2 * phi_bar
    out_ref[...] = phi1 / rho1 * model0 + phi2 / rho2 * search


def read(blocks_ref, tile_ref, sems, first):
    pieces = sems.shape[0]
    size = tile_ref.shape[0] // pieces
    return [
        pltpu.make_async_copy(
            blocks_ref.at[pl.ds(first + piece * size, size)],
            tile_ref.at[pl.ds(piece * size, size)],
            sems.at[piece],
        )
        for piece in range(pieces)
    ]


def load_first(
    live_ref,
    data_ref,
    rows_ref,
    cols_ref,
    blocks_ref,
    data_out,
    rows_out,
    cols_out,
    tile_ref,
    held_ref,
    small_sems,
    sems,
):
    small = [
        pltpu.make_async_copy(cols_ref, held_ref, small_sems.at[0]),
        pltpu.make_async_copy(rows_ref, rows_out, small_sems.at[1]),
        pltpu.make_async_copy(data_ref, data_out, small_sems.at[2]),
    ]
    large = read(blocks_ref, tile_ref, sems, 0)
    for copy in small + large:
        copy.start()
    small[0].wait()
    cols = held_ref[...]
    chunk = jnp.zeros_like(cols)
    for edge in range(CHUNK, CB, CHUNK):
        chunk += jnp.where(cols >= edge, 1, 0)
    half = jnp.where((chunk & 1) == (lax.axis_index("dp") & 1), 0, HALF)
    cols_out[...] = half + (chunk >> 1) * CHUNK + cols - chunk * CHUNK
    for copy in small[1:] + large:
        copy.wait()


def load_second(after_ref, blocks_ref, tile_ref, sems):
    large = read(blocks_ref, tile_ref, sems, blocks_ref.shape[0] - tile_ref.shape[0])
    for copy in large:
        copy.start()
    for copy in large:
        copy.wait()


def transpose(live_ref, after_ref, rows_ref, cols_ref, first_ref, second_ref, out_ref, pick_ref, hot_ref):
    pick_ref[...] = picker(cols_ref[...], CB, live_ref[0, 0])
    hot_ref[...] = adder(rows_ref[...], RB, live_ref[0, 0])
    base = 0
    for ref in (first_ref, second_ref):
        for slot in range(ref.shape[0]):
            out_ref[base + slot] = jnp.transpose(ref[slot])
        base += ref.shape[0]


def collect(own_ref, one_ref, two_ref, three_ref, after_ref, out_ref):
    size = own_ref.shape[0]
    for piece, ref in enumerate((own_ref, one_ref, two_ref, three_ref)):
        out_ref[piece * size : (piece + 1) * size, :] = ref[...]


SCALAR = pl.BlockSpec(memory_space=pltpu.SMEM)
VECTOR = pl.BlockSpec(memory_space=pltpu.VMEM)


def call(kernel, outs, vectors, scalars=(), slots=0):
    scratch = [pltpu.VMEM((slots, BS), BF16), pltpu.VMEM((slots, BS), F32)] if slots else []
    return pl.pallas_call(
        kernel,
        out_shape=[jax.ShapeDtypeStruct((rows, *(width or (BS,))), dtype) for rows, dtype, *width in outs],
        in_specs=[SCALAR] * len(scalars) + [VECTOR] * len(vectors),
        out_specs=[VECTOR] * len(outs),
        scratch_shapes=scratch,
        compiler_params=pltpu.CompilerParams(vmem_limit_bytes=16 * 2**20),
        name=kernel.__name__,
    )(*scalars, *vectors)


def body(rhs, blocks, block_rows, block_cols, counts):
    slots = blocks.shape[2]

    def over_core(x):
        return lax.ppermute(x, "dp", [(i, i ^ 1) for i in range(8)])

    def over_chips(x):
        steps = ((1, 3), (3, 1), (2, 2))
        return [
            lax.ppermute(x, "dp", [(i, (i >> 1 ^ step[i & 1]) * 2 + (i & 1)) for i in range(8)]) for step in steps
        ]

    def over_square(x, others):
        steps = zip(square(*others), square(*others[::-1]))
        return [
            lax.ppermute(
                x, ("dp", "mp"), [(i * 16 + j, i * 16 + (j ^ step[i & 1])) for i in range(8) for j in range(16)]
            )
            for step in steps
        ]

    def over_places(x, others):
        return [lax.ppermute(x, "mp", [(j, j ^ step) for j in range(16)]) for step in square(*others)]

    message = (HALF + EXTRA, BF16)
    scalar = (8, F32)
    model_outs = [(HALF, F32), message, scalar]

    lies = pl.BlockSpec(memory_space=pltpu.HBM)
    inputs = [
        pltpu.with_memory_space_constraint(x, pltpu.HBM) for x in (rhs, block_rows[0], block_cols[0], blocks[0, 0])
    ]
    early = slots * 3 // 8
    first_shape = pltpu.VMEM((early, BS, BS), BF16)
    second_shape = pltpu.VMEM((slots - early, BS, BS), BF16)
    params = pltpu.CompilerParams(vmem_limit_bytes=16 * 2**20)
    cost = pl.CostEstimate(flops=0, bytes_accessed=slots * BS * BS * 2, transcendentals=0)
    data, rows, cols, first = pl.pallas_call(
        load_first,
        out_shape=[
            jax.ShapeDtypeStruct(rhs.shape, F32),
            jax.ShapeDtypeStruct((1, slots), jnp.int32),
            jax.ShapeDtypeStruct((1, slots), jnp.int32),
            first_shape,
        ],
        in_specs=[SCALAR] + [lies] * 4,
        out_specs=[VECTOR] * 4,
        scratch_shapes=[
            pltpu.VMEM((1, slots), jnp.int32),
            pltpu.SemaphoreType.DMA((3,)),
            pltpu.SemaphoreType.DMA((LOADS,)),
        ],
        compiler_params=params,
        cost_estimate=cost,
        name="load_first",
    )(counts, *inputs)
    first = pltpu.with_memory_space_constraint(first, pltpu.VMEM)
    (quarter,) = call(collect, [(4 * SHARE, F32)], [data, *over_places(rhs, NEAR), first])
    second = pl.pallas_call(
        load_second,
        out_shape=second_shape,
        in_specs=[VECTOR, lies],
        out_specs=VECTOR,
        scratch_shapes=[pltpu.SemaphoreType.DMA((LOADS,))],
        compiler_params=params,
        cost_estimate=cost,
        name="load_second",
    )(quarter, inputs[-1])
    second = pltpu.with_memory_space_constraint(second, pltpu.VMEM)

    def forward_whole(own):
        (part,) = call(forward, [(RB + EXTRA, BF16)], [own, over_core(own), pick_cols, add_rows, turned], (), slots)
        (part,) = call(row_sum, [(RB + EXTRA, BF16)], [part, *over_square(part, NEAR)])
        return [part, *over_square(part, FAR)]

    def chips_whole(part):
        return [part, *over_chips(part)]

    data0, pick_rows, add_cols, keep, send = call(
        first_adjoint,
        [(RB, F32), (slots, BF16, RB), (CB, BF16, slots), (HALF, F32), message],
        [quarter, *over_places(quarter, FAR), rows, cols, first, second],
        [counts],
        slots,
    )
    (part,) = call(chip_sum, [message], [keep, send, over_core(send)])
    turned, pick_cols, add_rows = pl.pallas_call(
        transpose,
        out_shape=[
            pltpu.VMEM((slots, BS, BS), BF16),
            jax.ShapeDtypeStruct((slots, CB), BF16),
            jax.ShapeDtypeStruct((RB, slots), BF16),
        ],
        in_specs=[SCALAR] + [VECTOR] * 5,
        out_specs=[VECTOR] * 3,
        compiler_params=params,
        cost_estimate=cost,
        name="transpose",
    )(counts, part, rows, cols, first, second)
    turned = pltpu.with_memory_space_constraint(turned, pltpu.VMEM)
    model0, own, beta0 = call(first_model, model_outs, [*chips_whole(part), turned])
    data1, alpha0, keep, send = call(
        second_adjoint,
        [(RB, F32), scalar, (HALF, F32), message],
        [*forward_whole(own), data0, beta0, pick_rows, add_cols, first, second],
        (),
        slots,
    )
    (part,) = call(chip_sum, [message], [keep, send, over_core(send)])
    model1, own, beta1 = call(second_model, model_outs, [*chips_whole(part), model0, alpha0])
    alpha1, total = call(last_data, [scalar, scalar], [*forward_whole(own), data1, beta1])
    (total,) = call(add, [scalar], [total, over_core(total)])
    (out,) = call(
        finish,
        [(CHUNK, F32)],
        [total, *over_chips(total), beta0, alpha0, beta1, alpha1, model0, model1],
    )
    return out


def solution(mesh):
    placed = (
        P(("dp", "mp"), None),
        P("dp", "mp", None, None, None),
        P("dp", "mp", None),
        P("dp", "mp", None),
        P("dp", "mp"),
    )
    return jax.shard_map(
        body, mesh=mesh, in_specs=placed, out_specs=P(("mp", "dp"), None), check_vma=False
    )
```

```python
import functools

import jax
import jax.numpy as jnp
from jax import lax
from jax.experimental import pallas as pl
from jax.experimental.pallas import tpu as pltpu
from jax.sharding import PartitionSpec as P

BS = 128
RB = 512
CB = 768
HALF = CB // 2
CHUNK = 96
GROUP = 16
EXTRA = 16
LOADS = 8
SHARE = 32
NEAR = (1, 3)
FAR = (3, 1)
F32 = jnp.float32
BF16 = jnp.bfloat16


def square(other_x, other_y):
    return other_y, 4 * other_x, 4 * other_x + other_y


def split_rows(value):
    row = lax.broadcasted_iota(jnp.int32, (EXTRA, BS), 0)
    value = jnp.broadcast_to(value, (EXTRA, BS))
    high = value.astype(BF16).astype(F32)
    rest = value - high
    middle = rest.astype(BF16).astype(F32)
    low = rest - middle
    zero = jnp.zeros_like(value)
    return jnp.where(row == 0, high, jnp.where(row == 1, middle, jnp.where(row == 2, low, zero))).astype(BF16)


def joined_rows(rows):
    return jnp.sum(rows.astype(F32), axis=0, keepdims=True)


def square_sum(x):
    return jnp.sum(jnp.sum(x * x, axis=0, keepdims=True), axis=1, keepdims=True)


def column(index):
    pieces = []
    for start in range(0, index.shape[1], BS):
        row = jnp.broadcast_to(index[:, start : start + BS].astype(F32), (BS, BS))
        pieces.append(jnp.transpose(row))
    return jnp.concatenate(pieces, 0)


def picker(index, size, live):
    at = column(index)
    lane = lax.broadcasted_iota(jnp.int32, at.shape, 1)
    slot = lax.broadcasted_iota(jnp.int32, at.shape, 0)
    return jnp.concatenate(
        [
            jnp.where((at == (lane + start).astype(F32)) & (slot < live), 1.0, 0.0).astype(BF16)
            for start in range(0, size, BS)
        ],
        1,
    )


def adder(index, size, live):
    slots = index.shape[1]
    lane = lax.broadcasted_iota(jnp.int32, (size, slots), 1)
    row = lax.broadcasted_iota(jnp.int32, (size, slots), 0)
    return jnp.where((jnp.broadcast_to(index, (size, slots)) == row) & (lane < live), 1.0, 0.0).astype(BF16)


def gather(pick_ref, source, picked_ref):
    for start in range(0, picked_ref.shape[0], BS):
        piece = jnp.dot(pick_ref[start : start + BS, :], source, preferred_element_type=F32)
        picked_ref[start : start + BS, :] = piece.astype(BF16)


def scatter(products_ref, hot_ref):
    slots = products_ref.shape[0]
    total = 0.0
    for start in range(0, slots, 2 * BS):
        piece = slice(start, min(start + 2 * BS, slots))
        products = products_ref[piece, :]
        high = products.astype(BF16)
        low = (products - high.astype(F32)).astype(BF16)
        total += jnp.dot(hot_ref[:, piece], jnp.concatenate([high, low], 1), preferred_element_type=F32)
    return total[:, :BS] + total[:, BS:]


def spread(picked):
    row = lax.broadcasted_iota(jnp.int32, (GROUP, BS), 0)
    wide = picked.astype(F32)
    return jnp.concatenate([jnp.where(row == slot, wide, 0.0).astype(BF16) for slot in range(GROUP)], 1)


def multiply(blocks_refs, picked_ref, products_ref):
    def block(slot, size):
        for ref in blocks_refs:
            if slot < ref.shape[0]:
                return ref[slot : slot + size]
            slot -= ref.shape[0]

    slots = picked_ref.shape[0]
    singles = slots // 4
    groups = (slots - singles) // GROUP
    turned = []
    for start in range(0, singles, BS):
        rows = picked_ref[start : min(start + BS, singles), :].astype(F32)
        if rows.shape[0] < BS:
            rows = jnp.concatenate([rows, jnp.zeros((BS - rows.shape[0], BS), F32)], 0)
        turned.append(jnp.transpose(rows))
    for group in range(groups):
        start = singles + group * GROUP
        for single in range(singles * group // groups, singles * (group + 1) // groups):
            weights = jnp.broadcast_to(turned[single // BS][:, single % BS : single % BS + 1], (BS, BS))
            product = block(single, 1)[0].astype(F32) * weights
            products_ref[single : single + 1, :] = jnp.sum(product, axis=0, keepdims=True)
        tile = block(start, GROUP).reshape(GROUP * BS, BS)
        products_ref[start : start + GROUP, :] = jnp.dot(
            spread(picked_ref[start : start + GROUP, :]), tile, preferred_element_type=F32
        )


def adjoint_tail(data, pick_ref, hot_ref, blocks_refs, products_ref, send_ref, picked_ref):
    gather(pick_ref, data.astype(BF16), picked_ref)
    multiply(blocks_refs, picked_ref, products_ref)
    send_ref[:HALF, :] = scatter(products_ref, hot_ref.at[HALF:, :]).astype(BF16)
    send_ref[HALF:, :] = split_rows(square_sum(data))


def first_adjoint(
    live_ref,
    own_ref,
    one_ref,
    two_ref,
    three_ref,
    rows_ref,
    cols_ref,
    first_ref,
    second_ref,
    data_ref,
    pick_ref,
    hot_ref,
    products_ref,
    send_ref,
    picked_ref,
):
    near, far = square(*NEAR), square(*FAR)
    place = lax.axis_index("mp")
    for step, ref in zip((0, *far), (own_ref, one_ref, two_ref, three_ref)):
        for piece, hop in enumerate((0, *near)):
            at = pl.multiple_of((place ^ step ^ hop) * SHARE, SHARE)
            data_ref[pl.ds(at, SHARE), :] = ref[piece * SHARE : (piece + 1) * SHARE, :]
    live = live_ref[0, 0]
    pick_ref[...] = picker(rows_ref[...], RB, live)
    hot_ref[...] = adder(cols_ref[...], CB, live)
    blocks_refs = (first_ref, second_ref)
    adjoint_tail(data_ref[...], pick_ref, hot_ref, blocks_refs, products_ref, send_ref, picked_ref)


def forward_sum(own_ref, one_ref, two_ref, three_ref):
    parts = [ref[...].astype(F32) for ref in (own_ref, one_ref, two_ref, three_ref)]
    return (parts[0] + parts[1]) + (parts[2] + parts[3])


def next_data(own_ref, one_ref, two_ref, three_ref, data_ref, beta2_ref):
    whole = forward_sum(own_ref, one_ref, two_ref, three_ref)
    alpha2 = joined_rows(whole[RB:])
    alpha = jnp.sqrt(alpha2)
    beta = jnp.sqrt(beta2_ref[0:1, :])
    return whole[:RB] * (1.0 / alpha) - data_ref[...] * (alpha / beta), alpha2


def second_adjoint(
    own_ref,
    one_ref,
    two_ref,
    three_ref,
    data_ref,
    beta2_ref,
    pick_ref,
    hot_ref,
    first_ref,
    second_ref,
    next_ref,
    alpha2_ref,
    products_ref,
    send_ref,
    picked_ref,
):
    data, alpha2 = next_data(own_ref, one_ref, two_ref, three_ref, data_ref, beta2_ref)
    next_ref[...] = data
    alpha2_ref[...] = jnp.broadcast_to(alpha2, alpha2_ref.shape)
    blocks_refs = (first_ref, second_ref)
    adjoint_tail(
        data, pick_ref, hot_ref, blocks_refs, products_ref, send_ref, picked_ref
    )


def add_own(products_ref, hot_ref, keep_ref):
    keep_ref[...] = scatter(products_ref, hot_ref.at[:HALF, :])


def chip_sum(keep_ref, send_ref, got_ref, out_ref):
    out_ref[:HALF, :] = (keep_ref[...] + got_ref[:HALF, :].astype(F32)).astype(BF16)
    out_ref[HALF:, :] = split_rows(joined_rows(send_ref[HALF:, :]) + joined_rows(got_ref[HALF:, :]))


def model_sum(own_ref, one_ref, two_ref, three_ref):
    whole = forward_sum(own_ref, one_ref, two_ref, three_ref)
    return whole[:HALF], joined_rows(whole[HALF:])


def model_out(model, beta2, model_ref, send_ref, beta2_ref):
    model_ref[...] = model
    send_ref[:HALF, :] = model.astype(BF16)
    send_ref[HALF:, :] = split_rows(square_sum(model))
    beta2_ref[...] = jnp.broadcast_to(beta2, beta2_ref.shape)


def first_model(own_ref, one_ref, two_ref, three_ref, turned_ref, model_ref, send_ref, beta2_ref):
    total, beta2 = model_sum(own_ref, one_ref, two_ref, three_ref)
    model_out(total * (1.0 / jnp.sqrt(beta2)), beta2, model_ref, send_ref, beta2_ref)


def second_model(
    own_ref, one_ref, two_ref, three_ref, last_ref, alpha2_ref, model_ref, send_ref, beta2_ref
):
    total, beta2 = model_sum(own_ref, one_ref, two_ref, three_ref)
    beta = jnp.sqrt(beta2)
    alpha = jnp.sqrt(alpha2_ref[0:1, :])
    model_out(total * (1.0 / beta) - last_ref[...] * (beta / alpha), beta2, model_ref, send_ref, beta2_ref)


def forward(own_ref, got_ref, pick_ref, hot_ref, blocks_ref, out_ref, picked_ref, products_ref):
    model = jnp.concatenate([own_ref[:HALF, :], got_ref[:HALF, :]], 0)
    gather(pick_ref, model, picked_ref)
    multiply((blocks_ref,), picked_ref, products_ref)
    out_ref[:RB, :] = scatter(products_ref, hot_ref).astype(BF16)
    out_ref[RB:, :] = split_rows(joined_rows(own_ref[HALF:, :]) + joined_rows(got_ref[HALF:, :]))


def row_sum(own_ref, one_ref, two_ref, three_ref, out_ref):
    whole = forward_sum(own_ref, one_ref, two_ref, three_ref)
    out_ref[:RB, :] = whole[:RB].astype(BF16)
    out_ref[RB:, :] = split_rows(joined_rows(whole[RB:]))


def last_data(own_ref, one_ref, two_ref, three_ref, data_ref, beta2_ref, alpha2_ref, square_ref):
    data, alpha2 = next_data(own_ref, one_ref, two_ref, three_ref, data_ref, beta2_ref)
    alpha2_ref[...] = jnp.broadcast_to(alpha2, alpha2_ref.shape)
    square_ref[...] = jnp.broadcast_to(square_sum(data), square_ref.shape)


def add(own_ref, got_ref, out_ref):
    out_ref[...] = own_ref[...] + got_ref[...]


def finish(
    own_ref,
    one_ref,
    two_ref,
    three_ref,
    beta0_ref,
    alpha0_ref,
    beta1_ref,
    alpha1_ref,
    model0_ref,
    model1_ref,
    out_ref,
):
    beta0 = jnp.sqrt(beta0_ref[0:1, :])
    alpha0 = jnp.sqrt(alpha0_ref[0:1, :])
    beta1 = jnp.sqrt(beta1_ref[0:1, :])
    alpha1 = jnp.sqrt(alpha1_ref[0:1, :])
    beta2 = jnp.sqrt(forward_sum(own_ref, one_ref, two_ref, three_ref)[0:1, :])
    chunk = pl.ds(pl.multiple_of((lax.axis_index("dp") >> 1) * CHUNK, CHUNK), CHUNK)
    model0 = model0_ref[chunk, :] / alpha0
    model1 = model1_ref[chunk, :] / alpha1
    rho1 = jnp.sqrt(alpha0 * alpha0 + beta1 * beta1)
    cosine = alpha0 / rho1
    sine = beta1 / rho1
    theta = sine * alpha1
    rho_bar = -cosine * alpha1
    phi1 = cosine * beta0
    phi_bar = sine * beta0
    search = model1 - theta / rho1 * model0
    rho2 = jnp.sqrt(rho_bar * rho_bar + beta2 * beta2)
    phi2 = rho_bar / rho2 * phi_bar
    out_ref[...] = phi1 / rho1 * model0 + phi2 / rho2 * search


def read(blocks_ref, tile_ref, sems, first):
    pieces = sems.shape[0]
    size = tile_ref.shape[0] // pieces
    return [
        pltpu.make_async_copy(
            blocks_ref.at[pl.ds(first + piece * size, size)],
            tile_ref.at[pl.ds(piece * size, size)],
            sems.at[piece],
        )
        for piece in range(pieces)
    ]


def load_first(
    live_ref,
    data_ref,
    rows_ref,
    cols_ref,
    blocks_ref,
    data_out,
    rows_out,
    cols_out,
    tile_ref,
    held_ref,
    small_sems,
    sems,
):
    small = [
        pltpu.make_async_copy(cols_ref, held_ref, small_sems.at[0]),
        pltpu.make_async_copy(rows_ref, rows_out, small_sems.at[1]),
        pltpu.make_async_copy(data_ref, data_out, small_sems.at[2]),
    ]
    large = read(blocks_ref, tile_ref, sems, 0)
    for copy in small + large:
        copy.start()
    small[0].wait()
    cols = held_ref[...]
    chunk = jnp.zeros_like(cols)
    for edge in range(CHUNK, CB, CHUNK):
        chunk += jnp.where(cols >= edge, 1, 0)
    half = jnp.where((chunk & 1) == (lax.axis_index("dp") & 1), 0, HALF)
    cols_out[...] = half + (chunk >> 1) * CHUNK + cols - chunk * CHUNK
    for copy in small[1:] + large:
        copy.wait()


def load_second(after_ref, blocks_ref, tile_ref, sems):
    large = read(blocks_ref, tile_ref, sems, blocks_ref.shape[0] - tile_ref.shape[0])
    for copy in large:
        copy.start()
    for copy in large:
        copy.wait()


def transpose(live_ref, after_ref, rows_ref, cols_ref, first_ref, second_ref, out_ref, pick_ref, hot_ref):
    pick_ref[...] = picker(cols_ref[...], CB, live_ref[0, 0])
    hot_ref[...] = adder(rows_ref[...], RB, live_ref[0, 0])
    base = 0
    for ref in (first_ref, second_ref):
        for slot in range(ref.shape[0]):
            out_ref[base + slot] = jnp.transpose(ref[slot])
        base += ref.shape[0]


def collect(own_ref, one_ref, two_ref, three_ref, after_ref, out_ref):
    size = own_ref.shape[0]
    for piece, ref in enumerate((own_ref, one_ref, two_ref, three_ref)):
        out_ref[piece * size : (piece + 1) * size, :] = ref[...]


SCALAR = pl.BlockSpec(memory_space=pltpu.SMEM)
VECTOR = pl.BlockSpec(memory_space=pltpu.VMEM)


def call(kernel, outs, vectors, scalars=(), slots=0, held=(), work=0):
    scratch = [pltpu.VMEM((slots, BS), dtype) for dtype in held]
    return pl.pallas_call(
        kernel,
        out_shape=[jax.ShapeDtypeStruct((rows, *(width or (BS,))), dtype) for rows, dtype, *width in outs],
        in_specs=[SCALAR] * len(scalars) + [VECTOR] * len(vectors),
        out_specs=[VECTOR] * len(outs),
        scratch_shapes=scratch,
        compiler_params=pltpu.CompilerParams(vmem_limit_bytes=16 * 2**20),
        cost_estimate=pl.CostEstimate(flops=0, bytes_accessed=work, transcendentals=0) if work else None,
        name=kernel.__name__,
    )(*scalars, *vectors)


def body(rhs, blocks, block_rows, block_cols, counts):
    slots = blocks.shape[2]

    def over_core(x):
        return lax.ppermute(x, "dp", [(i, i ^ 1) for i in range(8)])

    def over_chips(x):
        steps = ((1, 3), (3, 1), (2, 2))
        return [
            lax.ppermute(x, "dp", [(i, (i >> 1 ^ step[i & 1]) * 2 + (i & 1)) for i in range(8)]) for step in steps
        ]

    def over_square(x, others):
        steps = zip(square(*others), square(*others[::-1]))
        return [
            lax.ppermute(
                x, ("dp", "mp"), [(i * 16 + j, i * 16 + (j ^ step[i & 1])) for i in range(8) for j in range(16)]
            )
            for step in steps
        ]

    def over_places(x, others):
        return [lax.ppermute(x, "mp", [(j, j ^ step) for j in range(16)]) for step in square(*others)]

    message = (HALF + EXTRA, BF16)
    scalar = (8, F32)
    model_outs = [(HALF, F32), message, scalar]

    lies = pl.BlockSpec(memory_space=pltpu.HBM)
    inputs = [
        pltpu.with_memory_space_constraint(x, pltpu.HBM) for x in (rhs, block_rows[0], block_cols[0], blocks[0, 0])
    ]
    early = slots * 3 // 8
    first_shape = pltpu.VMEM((early, BS, BS), BF16)
    second_shape = pltpu.VMEM((slots - early, BS, BS), BF16)
    params = pltpu.CompilerParams(vmem_limit_bytes=16 * 2**20)
    cost = pl.CostEstimate(flops=0, bytes_accessed=slots * BS * BS * 2, transcendentals=0)
    data, rows, cols, first = pl.pallas_call(
        load_first,
        out_shape=[
            jax.ShapeDtypeStruct(rhs.shape, F32),
            jax.ShapeDtypeStruct((1, slots), jnp.int32),
            jax.ShapeDtypeStruct((1, slots), jnp.int32),
            first_shape,
        ],
        in_specs=[SCALAR] + [lies] * 4,
        out_specs=[VECTOR] * 4,
        scratch_shapes=[
            pltpu.VMEM((1, slots), jnp.int32),
            pltpu.SemaphoreType.DMA((3,)),
            pltpu.SemaphoreType.DMA((LOADS,)),
        ],
        compiler_params=params,
        cost_estimate=cost,
        name="load_first",
    )(counts, *inputs)
    first = pltpu.with_memory_space_constraint(first, pltpu.VMEM)
    (quarter,) = call(collect, [(4 * SHARE, F32)], [data, *over_places(rhs, NEAR), first])
    second = pl.pallas_call(
        load_second,
        out_shape=second_shape,
        in_specs=[VECTOR, lies],
        out_specs=VECTOR,
        scratch_shapes=[pltpu.SemaphoreType.DMA((LOADS,))],
        compiler_params=params,
        cost_estimate=cost,
        name="load_second",
    )(quarter, inputs[-1])
    second = pltpu.with_memory_space_constraint(second, pltpu.VMEM)

    def forward_whole(own):
        (part,) = call(forward, [(RB + EXTRA, BF16)], [own, over_core(own), pick_cols, add_rows, turned], (), slots, (BF16, F32))
        (part,) = call(row_sum, [(RB + EXTRA, BF16)], [part, *over_square(part, NEAR)])
        return [part, *over_square(part, FAR)]

    def chips_whole(part):
        return [part, *over_chips(part)]

    data0, pick_rows, add_cols, products, send = call(
        first_adjoint,
        [(RB, F32), (slots, BF16, RB), (CB, BF16, slots), (slots, F32), message],
        [quarter, *over_places(quarter, FAR), rows, cols, first, second],
        [counts],
        slots,
        (BF16,),
    )
    got = over_core(send)
    (keep,) = call(add_own, [(HALF, F32)], [products, add_cols], work=CB * slots * 2)
    (part,) = call(chip_sum, [message], [keep, send, got])
    turned, pick_cols, add_rows = pl.pallas_call(
        transpose,
        out_shape=[
            pltpu.VMEM((slots, BS, BS), BF16),
            jax.ShapeDtypeStruct((slots, CB), BF16),
            jax.ShapeDtypeStruct((RB, slots), BF16),
        ],
        in_specs=[SCALAR] + [VECTOR] * 5,
        out_specs=[VECTOR] * 3,
        compiler_params=params,
        cost_estimate=cost,
        name="transpose",
    )(counts, part, rows, cols, first, second)
    turned = pltpu.with_memory_space_constraint(turned, pltpu.VMEM)
    model0, own, beta0 = call(first_model, model_outs, [*chips_whole(part), turned])
    data1, alpha0, products, send = call(
        second_adjoint,
        [(RB, F32), scalar, (slots, F32), message],
        [*forward_whole(own), data0, beta0, pick_rows, add_cols, first, second],
        (),
        slots,
        (BF16,),
    )
    got = over_core(send)
    (keep,) = call(add_own, [(HALF, F32)], [products, add_cols], work=CB * slots * 2)
    (part,) = call(chip_sum, [message], [keep, send, got])
    model1, own, beta1 = call(second_model, model_outs, [*chips_whole(part), model0, alpha0])
    alpha1, total = call(last_data, [scalar, scalar], [*forward_whole(own), data1, beta1])
    (total,) = call(add, [scalar], [total, over_core(total)])
    (out,) = call(
        finish,
        [(CHUNK, F32)],
        [total, *over_chips(total), beta0, alpha0, beta1, alpha1, model0, model1],
    )
    return out


def solution(mesh):
    placed = (
        P(("dp", "mp"), None),
        P("dp", "mp", None, None, None),
        P("dp", "mp", None),
        P("dp", "mp", None),
        P("dp", "mp"),
    )
    return jax.shard_map(
        body, mesh=mesh, in_specs=placed, out_specs=P(("mp", "dp"), None), check_vma=False
    )
```

```python
import functools

import jax
import jax.numpy as jnp
from jax import lax
from jax.experimental import pallas as pl
from jax.experimental.pallas import tpu as pltpu
from jax.sharding import PartitionSpec as P

BS = 128
RB = 512
CB = 768
HALF = CB // 2
CHUNK = 96
GROUP = 16
EXTRA = 16
LOADS = 8
SHARE = 32
NEAR = (1, 3)
FAR = (3, 1)
F32 = jnp.float32
BF16 = jnp.bfloat16


def square(other_x, other_y):
    return other_y, 4 * other_x, 4 * other_x + other_y


def split_rows(value):
    row = lax.broadcasted_iota(jnp.int32, (EXTRA, BS), 0)
    value = jnp.broadcast_to(value, (EXTRA, BS))
    high = value.astype(BF16).astype(F32)
    rest = value - high
    middle = rest.astype(BF16).astype(F32)
    low = rest - middle
    zero = jnp.zeros_like(value)
    return jnp.where(row == 0, high, jnp.where(row == 1, middle, jnp.where(row == 2, low, zero))).astype(BF16)


def joined_rows(rows):
    return jnp.sum(rows.astype(F32), axis=0, keepdims=True)


def square_sum(x):
    return jnp.sum(jnp.sum(x * x, axis=0, keepdims=True), axis=1, keepdims=True)


def column(index):
    pieces = []
    for start in range(0, index.shape[1], BS):
        row = jnp.broadcast_to(index[:, start : start + BS].astype(F32), (BS, BS))
        pieces.append(jnp.transpose(row))
    return jnp.concatenate(pieces, 0)


def picker(index, size, live):
    at = column(index)
    lane = lax.broadcasted_iota(jnp.int32, at.shape, 1)
    slot = lax.broadcasted_iota(jnp.int32, at.shape, 0)
    return jnp.concatenate(
        [
            jnp.where((at == (lane + start).astype(F32)) & (slot < live), 1.0, 0.0).astype(BF16)
            for start in range(0, size, BS)
        ],
        1,
    )


def adder(index, size, live):
    slots = index.shape[1]
    lane = lax.broadcasted_iota(jnp.int32, (size, slots), 1)
    row = lax.broadcasted_iota(jnp.int32, (size, slots), 0)
    return jnp.where((jnp.broadcast_to(index, (size, slots)) == row) & (lane < live), 1.0, 0.0).astype(BF16)


def gather(pick_ref, source, picked_ref, also_ref=None):
    for start in range(0, picked_ref.shape[0], BS):
        rows = slice(start, start + BS)
        piece = jnp.dot(pick_ref[rows, :], source, preferred_element_type=F32)
        if also_ref is not None:
            piece += also_ref[rows, :].astype(F32)
        picked_ref[rows, :] = piece.astype(BF16)


def scatter(products_ref, hot_ref):
    slots = products_ref.shape[0]
    total = 0.0
    for start in range(0, slots, 2 * BS):
        piece = slice(start, min(start + 2 * BS, slots))
        products = products_ref[piece, :]
        high = products.astype(BF16)
        low = (products - high.astype(F32)).astype(BF16)
        total += jnp.dot(hot_ref[:, piece], jnp.concatenate([high, low], 1), preferred_element_type=F32)
    return total[:, :BS] + total[:, BS:]


def spread(picked):
    row = lax.broadcasted_iota(jnp.int32, (GROUP, BS), 0)
    wide = picked.astype(F32)
    return jnp.concatenate([jnp.where(row == slot, wide, 0.0).astype(BF16) for slot in range(GROUP)], 1)


def multiply(blocks_refs, picked_ref, products_ref):
    def block(slot, size):
        for ref in blocks_refs:
            if slot < ref.shape[0]:
                return ref[slot : slot + size]
            slot -= ref.shape[0]

    slots = picked_ref.shape[0]
    singles = slots // 4
    groups = (slots - singles) // GROUP
    turned = []
    for start in range(0, singles, BS):
        rows = picked_ref[start : min(start + BS, singles), :].astype(F32)
        if rows.shape[0] < BS:
            rows = jnp.concatenate([rows, jnp.zeros((BS - rows.shape[0], BS), F32)], 0)
        turned.append(jnp.transpose(rows))
    for group in range(groups):
        start = singles + group * GROUP
        for single in range(singles * group // groups, singles * (group + 1) // groups):
            weights = jnp.broadcast_to(turned[single // BS][:, single % BS : single % BS + 1], (BS, BS))
            product = block(single, 1)[0].astype(F32) * weights
            products_ref[single : single + 1, :] = jnp.sum(product, axis=0, keepdims=True)
        tile = block(start, GROUP).reshape(GROUP * BS, BS)
        products_ref[start : start + GROUP, :] = jnp.dot(
            spread(picked_ref[start : start + GROUP, :]), tile, preferred_element_type=F32
        )


def adjoint_tail(data, pick_ref, hot_ref, blocks_refs, products_ref, send_ref, picked_ref):
    gather(pick_ref, data.astype(BF16), picked_ref)
    multiply(blocks_refs, picked_ref, products_ref)
    send_ref[:HALF, :] = scatter(products_ref, hot_ref.at[HALF:, :]).astype(BF16)
    send_ref[HALF:, :] = split_rows(square_sum(data))


def first_adjoint(
    live_ref,
    own_ref,
    one_ref,
    two_ref,
    three_ref,
    rows_ref,
    cols_ref,
    first_ref,
    second_ref,
    data_ref,
    pick_ref,
    hot_ref,
    products_ref,
    send_ref,
    picked_ref,
):
    near, far = square(*NEAR), square(*FAR)
    place = lax.axis_index("mp")
    for step, ref in zip((0, *far), (own_ref, one_ref, two_ref, three_ref)):
        for piece, hop in enumerate((0, *near)):
            at = pl.multiple_of((place ^ step ^ hop) * SHARE, SHARE)
            data_ref[pl.ds(at, SHARE), :] = ref[piece * SHARE : (piece + 1) * SHARE, :]
    live = live_ref[0, 0]
    pick_ref[...] = picker(rows_ref[...], RB, live)
    hot_ref[...] = adder(cols_ref[...], CB, live)
    blocks_refs = (first_ref, second_ref)
    adjoint_tail(data_ref[...], pick_ref, hot_ref, blocks_refs, products_ref, send_ref, picked_ref)


def forward_sum(own_ref, one_ref, two_ref, three_ref):
    parts = [ref[...].astype(F32) for ref in (own_ref, one_ref, two_ref, three_ref)]
    return (parts[0] + parts[1]) + (parts[2] + parts[3])


def next_data(own_ref, one_ref, two_ref, three_ref, data_ref, beta2_ref):
    whole = forward_sum(own_ref, one_ref, two_ref, three_ref)
    alpha2 = joined_rows(whole[RB:])
    alpha = jnp.sqrt(alpha2)
    beta = jnp.sqrt(beta2_ref[0:1, :])
    return whole[:RB] * (1.0 / alpha) - data_ref[...] * (alpha / beta), alpha2


def second_adjoint(
    own_ref,
    one_ref,
    two_ref,
    three_ref,
    data_ref,
    beta2_ref,
    pick_ref,
    hot_ref,
    first_ref,
    second_ref,
    next_ref,
    alpha2_ref,
    products_ref,
    send_ref,
    picked_ref,
):
    data, alpha2 = next_data(own_ref, one_ref, two_ref, three_ref, data_ref, beta2_ref)
    next_ref[...] = data
    alpha2_ref[...] = jnp.broadcast_to(alpha2, alpha2_ref.shape)
    blocks_refs = (first_ref, second_ref)
    adjoint_tail(
        data, pick_ref, hot_ref, blocks_refs, products_ref, send_ref, picked_ref
    )


def add_own(products_ref, hot_ref, keep_ref):
    keep_ref[...] = scatter(products_ref, hot_ref.at[:HALF, :])


def chip_sum(keep_ref, send_ref, got_ref, out_ref):
    out_ref[:HALF, :] = (keep_ref[...] + got_ref[:HALF, :].astype(F32)).astype(BF16)
    out_ref[HALF:, :] = split_rows(joined_rows(send_ref[HALF:, :]) + joined_rows(got_ref[HALF:, :]))


def model_sum(own_ref, one_ref, two_ref, three_ref):
    whole = forward_sum(own_ref, one_ref, two_ref, three_ref)
    return whole[:HALF], joined_rows(whole[HALF:])


def model_out(model, beta2, model_ref, send_ref, beta2_ref):
    model_ref[...] = model
    send_ref[:HALF, :] = model.astype(BF16)
    send_ref[HALF:, :] = split_rows(square_sum(model))
    beta2_ref[...] = jnp.broadcast_to(beta2, beta2_ref.shape)


def first_model(own_ref, one_ref, two_ref, three_ref, turned_ref, model_ref, send_ref, beta2_ref):
    total, beta2 = model_sum(own_ref, one_ref, two_ref, three_ref)
    model_out(total * (1.0 / jnp.sqrt(beta2)), beta2, model_ref, send_ref, beta2_ref)


def second_model(
    own_ref, one_ref, two_ref, three_ref, last_ref, alpha2_ref, model_ref, send_ref, beta2_ref
):
    total, beta2 = model_sum(own_ref, one_ref, two_ref, three_ref)
    beta = jnp.sqrt(beta2)
    alpha = jnp.sqrt(alpha2_ref[0:1, :])
    model_out(total * (1.0 / beta) - last_ref[...] * (beta / alpha), beta2, model_ref, send_ref, beta2_ref)


def pick_own(own_ref, pick_ref, out_ref):
    gather(pick_ref.at[:, :HALF], own_ref[:HALF, :], out_ref)


def forward(own_ref, got_ref, mine_ref, pick_ref, hot_ref, blocks_ref, out_ref, picked_ref, products_ref):
    gather(pick_ref.at[:, HALF:], got_ref[:HALF, :], picked_ref, mine_ref)
    multiply((blocks_ref,), picked_ref, products_ref)
    out_ref[:RB, :] = scatter(products_ref, hot_ref).astype(BF16)
    out_ref[RB:, :] = split_rows(joined_rows(own_ref[HALF:, :]) + joined_rows(got_ref[HALF:, :]))


def row_sum(own_ref, one_ref, two_ref, three_ref, out_ref):
    whole = forward_sum(own_ref, one_ref, two_ref, three_ref)
    out_ref[:RB, :] = whole[:RB].astype(BF16)
    out_ref[RB:, :] = split_rows(joined_rows(whole[RB:]))


def last_data(own_ref, one_ref, two_ref, three_ref, data_ref, beta2_ref, alpha2_ref, square_ref):
    data, alpha2 = next_data(own_ref, one_ref, two_ref, three_ref, data_ref, beta2_ref)
    alpha2_ref[...] = jnp.broadcast_to(alpha2, alpha2_ref.shape)
    square_ref[...] = jnp.broadcast_to(square_sum(data), square_ref.shape)


def add(own_ref, got_ref, out_ref):
    out_ref[...] = own_ref[...] + got_ref[...]


def finish(
    own_ref,
    one_ref,
    two_ref,
    three_ref,
    beta0_ref,
    alpha0_ref,
    beta1_ref,
    alpha1_ref,
    model0_ref,
    model1_ref,
    out_ref,
):
    beta0 = jnp.sqrt(beta0_ref[0:1, :])
    alpha0 = jnp.sqrt(alpha0_ref[0:1, :])
    beta1 = jnp.sqrt(beta1_ref[0:1, :])
    alpha1 = jnp.sqrt(alpha1_ref[0:1, :])
    beta2 = jnp.sqrt(forward_sum(own_ref, one_ref, two_ref, three_ref)[0:1, :])
    chunk = pl.ds(pl.multiple_of((lax.axis_index("dp") >> 1) * CHUNK, CHUNK), CHUNK)
    model0 = model0_ref[chunk, :] / alpha0
    model1 = model1_ref[chunk, :] / alpha1
    rho1 = jnp.sqrt(alpha0 * alpha0 + beta1 * beta1)
    cosine = alpha0 / rho1
    sine = beta1 / rho1
    theta = sine * alpha1
    rho_bar = -cosine * alpha1
    phi1 = cosine * beta0
    phi_bar = sine * beta0
    search = model1 - theta / rho1 * model0
    rho2 = jnp.sqrt(rho_bar * rho_bar + beta2 * beta2)
    phi2 = rho_bar / rho2 * phi_bar
    out_ref[...] = phi1 / rho1 * model0 + phi2 / rho2 * search


def read(blocks_ref, tile_ref, sems, first):
    pieces = sems.shape[0]
    size = tile_ref.shape[0] // pieces
    return [
        pltpu.make_async_copy(
            blocks_ref.at[pl.ds(first + piece * size, size)],
            tile_ref.at[pl.ds(piece * size, size)],
            sems.at[piece],
        )
        for piece in range(pieces)
    ]


def load_first(
    live_ref,
    data_ref,
    rows_ref,
    cols_ref,
    blocks_ref,
    data_out,
    rows_out,
    cols_out,
    tile_ref,
    held_ref,
    small_sems,
    sems,
):
    small = [
        pltpu.make_async_copy(cols_ref, held_ref, small_sems.at[0]),
        pltpu.make_async_copy(rows_ref, rows_out, small_sems.at[1]),
        pltpu.make_async_copy(data_ref, data_out, small_sems.at[2]),
    ]
    large = read(blocks_ref, tile_ref, sems, 0)
    for copy in small + large:
        copy.start()
    small[0].wait()
    cols = held_ref[...]
    chunk = jnp.zeros_like(cols)
    for edge in range(CHUNK, CB, CHUNK):
        chunk += jnp.where(cols >= edge, 1, 0)
    half = jnp.where((chunk & 1) == (lax.axis_index("dp") & 1), 0, HALF)
    cols_out[...] = half + (chunk >> 1) * CHUNK + cols - chunk * CHUNK
    for copy in small[1:] + large:
        copy.wait()


def load_second(after_ref, blocks_ref, tile_ref, sems):
    large = read(blocks_ref, tile_ref, sems, blocks_ref.shape[0] - tile_ref.shape[0])
    for copy in large:
        copy.start()
    for copy in large:
        copy.wait()


def transpose(live_ref, after_ref, rows_ref, cols_ref, first_ref, second_ref, out_ref, pick_ref, hot_ref):
    pick_ref[...] = picker(cols_ref[...], CB, live_ref[0, 0])
    hot_ref[...] = adder(rows_ref[...], RB, live_ref[0, 0])
    base = 0
    for ref in (first_ref, second_ref):
        for slot in range(ref.shape[0]):
            out_ref[base + slot] = jnp.transpose(ref[slot])
        base += ref.shape[0]


def collect(own_ref, one_ref, two_ref, three_ref, after_ref, out_ref):
    size = own_ref.shape[0]
    for piece, ref in enumerate((own_ref, one_ref, two_ref, three_ref)):
        out_ref[piece * size : (piece + 1) * size, :] = ref[...]


SCALAR = pl.BlockSpec(memory_space=pltpu.SMEM)
VECTOR = pl.BlockSpec(memory_space=pltpu.VMEM)


def call(kernel, outs, vectors, scalars=(), slots=0, held=(), work=0):
    scratch = [pltpu.VMEM((slots, BS), dtype) for dtype in held]
    return pl.pallas_call(
        kernel,
        out_shape=[jax.ShapeDtypeStruct((rows, *(width or (BS,))), dtype) for rows, dtype, *width in outs],
        in_specs=[SCALAR] * len(scalars) + [VECTOR] * len(vectors),
        out_specs=[VECTOR] * len(outs),
        scratch_shapes=scratch,
        compiler_params=pltpu.CompilerParams(vmem_limit_bytes=16 * 2**20),
        cost_estimate=pl.CostEstimate(flops=0, bytes_accessed=work, transcendentals=0) if work else None,
        name=kernel.__name__,
    )(*scalars, *vectors)


def body(rhs, blocks, block_rows, block_cols, counts):
    slots = blocks.shape[2]

    def over_core(x):
        return lax.ppermute(x, "dp", [(i, i ^ 1) for i in range(8)])

    def over_chips(x):
        steps = ((1, 3), (3, 1), (2, 2))
        return [
            lax.ppermute(x, "dp", [(i, (i >> 1 ^ step[i & 1]) * 2 + (i & 1)) for i in range(8)]) for step in steps
        ]

    def over_square(x, others):
        steps = zip(square(*others), square(*others[::-1]))
        return [
            lax.ppermute(
                x, ("dp", "mp"), [(i * 16 + j, i * 16 + (j ^ step[i & 1])) for i in range(8) for j in range(16)]
            )
            for step in steps
        ]

    def over_places(x, others):
        return [lax.ppermute(x, "mp", [(j, j ^ step) for j in range(16)]) for step in square(*others)]

    message = (HALF + EXTRA, BF16)
    scalar = (8, F32)
    model_outs = [(HALF, F32), message, scalar]

    lies = pl.BlockSpec(memory_space=pltpu.HBM)
    inputs = [
        pltpu.with_memory_space_constraint(x, pltpu.HBM) for x in (rhs, block_rows[0], block_cols[0], blocks[0, 0])
    ]
    early = slots * 3 // 8
    first_shape = pltpu.VMEM((early, BS, BS), BF16)
    second_shape = pltpu.VMEM((slots - early, BS, BS), BF16)
    params = pltpu.CompilerParams(vmem_limit_bytes=16 * 2**20)
    cost = pl.CostEstimate(flops=0, bytes_accessed=slots * BS * BS * 2, transcendentals=0)
    data, rows, cols, first = pl.pallas_call(
        load_first,
        out_shape=[
            jax.ShapeDtypeStruct(rhs.shape, F32),
            jax.ShapeDtypeStruct((1, slots), jnp.int32),
            jax.ShapeDtypeStruct((1, slots), jnp.int32),
            first_shape,
        ],
        in_specs=[SCALAR] + [lies] * 4,
        out_specs=[VECTOR] * 4,
        scratch_shapes=[
            pltpu.VMEM((1, slots), jnp.int32),
            pltpu.SemaphoreType.DMA((3,)),
            pltpu.SemaphoreType.DMA((LOADS,)),
        ],
        compiler_params=params,
        cost_estimate=cost,
        name="load_first",
    )(counts, *inputs)
    first = pltpu.with_memory_space_constraint(first, pltpu.VMEM)
    (quarter,) = call(collect, [(4 * SHARE, F32)], [data, *over_places(rhs, NEAR), first])
    second = pl.pallas_call(
        load_second,
        out_shape=second_shape,
        in_specs=[VECTOR, lies],
        out_specs=VECTOR,
        scratch_shapes=[pltpu.SemaphoreType.DMA((LOADS,))],
        compiler_params=params,
        cost_estimate=cost,
        name="load_second",
    )(quarter, inputs[-1])
    second = pltpu.with_memory_space_constraint(second, pltpu.VMEM)

    def forward_whole(own):
        got = over_core(own)
        (mine,) = call(pick_own, [(slots, BF16)], [own, pick_cols], work=CB * slots * 2)
        inputs = [own, got, mine, pick_cols, add_rows, turned]
        (part,) = call(forward, [(RB + EXTRA, BF16)], inputs, (), slots, (BF16, F32))
        (part,) = call(row_sum, [(RB + EXTRA, BF16)], [part, *over_square(part, NEAR)])
        return [part, *over_square(part, FAR)]

    def chips_whole(part):
        return [part, *over_chips(part)]

    data0, pick_rows, add_cols, products, send = call(
        first_adjoint,
        [(RB, F32), (slots, BF16, RB), (CB, BF16, slots), (slots, F32), message],
        [quarter, *over_places(quarter, FAR), rows, cols, first, second],
        [counts],
        slots,
        (BF16,),
    )
    got = over_core(send)
    (keep,) = call(add_own, [(HALF, F32)], [products, add_cols], work=CB * slots * 2)
    (part,) = call(chip_sum, [message], [keep, send, got])
    turned, pick_cols, add_rows = pl.pallas_call(
        transpose,
        out_shape=[
            pltpu.VMEM((slots, BS, BS), BF16),
            jax.ShapeDtypeStruct((slots, CB), BF16),
            jax.ShapeDtypeStruct((RB, slots), BF16),
        ],
        in_specs=[SCALAR] + [VECTOR] * 5,
        out_specs=[VECTOR] * 3,
        compiler_params=params,
        cost_estimate=cost,
        name="transpose",
    )(counts, part, rows, cols, first, second)
    turned = pltpu.with_memory_space_constraint(turned, pltpu.VMEM)
    model0, own, beta0 = call(first_model, model_outs, [*chips_whole(part), turned])
    data1, alpha0, products, send = call(
        second_adjoint,
        [(RB, F32), scalar, (slots, F32), message],
        [*forward_whole(own), data0, beta0, pick_rows, add_cols, first, second],
        (),
        slots,
        (BF16,),
    )
    got = over_core(send)
    (keep,) = call(add_own, [(HALF, F32)], [products, add_cols], work=CB * slots * 2)
    (part,) = call(chip_sum, [message], [keep, send, got])
    model1, own, beta1 = call(second_model, model_outs, [*chips_whole(part), model0, alpha0])
    alpha1, total = call(last_data, [scalar, scalar], [*forward_whole(own), data1, beta1])
    (total,) = call(add, [scalar], [total, over_core(total)])
    (out,) = call(
        finish,
        [(CHUNK, F32)],
        [total, *over_chips(total), beta0, alpha0, beta1, alpha1, model0, model1],
    )
    return out


def solution(mesh):
    placed = (
        P(("dp", "mp"), None),
        P("dp", "mp", None, None, None),
        P("dp", "mp", None),
        P("dp", "mp", None),
        P("dp", "mp"),
    )
    return jax.shard_map(
        body, mesh=mesh, in_specs=placed, out_specs=P(("mp", "dp"), None), check_vma=False
    )
```
